256 devices in a mesh: rep: 8 (over x, y_hi), fsdp: 32 (over z, y_lo, core).
Axes of the slice: x: 4, y: 4 (y_hi: 2, y_lo: 2; y = y_hi * 2 + y_lo), z: 8, core: 2. Of those that a mesh axis runs over, the one named last changes fastest.
Arguments:
- activations: bfloat16 [8, 24576, 6144], P('rep', 'fsdp'), may hold values from -6 to 6
- out_grads: bfloat16 [8, 24576, 512], P('rep', 'fsdp'), may hold values from -0.0390625 to 0.0390625
- momentum: float32 [8, 6144, 512], P('rep', 'fsdp'), may hold values from -6 to 6
- indices: int32 [8, 96, 8, 128], P('rep', 'fsdp'), may hold values from 0 to 4095, as said below
- counts: int32 [8], P('rep'), may hold values from 64 to 128, as said below
Outputs:
- new_momentum: float32 [8, 6144, 512], P('rep', 'fsdp')
- step_dir: float32 [6144, 512], P('fsdp')
The draws below stay inside these ranges and needn't reach their ends.
Inputs may be any that keep to these rules, and one draw needn't show every extreme that they name: `indices`: in each replica's list for one tile the 128 entries are distinct; only the first counts[r] slots of replica r are in use, the others hold further distinct positions that are not chosen. `counts`: the same count holds for every tile of one replica; some replica uses all 128 slots.
All inputs are finite; a program needn't handle non-finite values.
Results may differ from the reference program's by a relative error of at most 0.0003.
Values may be sent and summed in bfloat16 or wider, within the bound.
No kernel may reach another device: no remote copies, remote signals or barrier semaphores. Data moves between devices by JAX's collectives and lax.ppermute only.
A program may use at most 192 MiB of HBM per device.

```python
import math
import jax
import jax.numpy as jnp
from jax import lax

D = 6144
LAT = 512
CH = 64
SLOTS = 128
REPS = 8
TOKENS = 24576


def draw_counts(key, part):
    key = jax.random.fold_in(key, 11)
    first, second = jax.random.split(key)
    drawn = jax.random.randint(first, (REPS,), SLOTS // 2, SLOTS + 1, dtype=jnp.int32)
    chosen = jax.random.randint(second, (), 0, REPS, dtype=jnp.int32)
    return jnp.where(jnp.arange(REPS, dtype=jnp.int32) == chosen, SLOTS, drawn).astype(jnp.int32)


def draw_indices(key, part):
    key = jax.random.fold_in(key, 23)
    tile_count = REPS * (D // CH) * (LAT // CH)
    flat_size = CH * CH
    scores = jax.random.randint(key, (tile_count, flat_size), 0, 262144, dtype=jnp.int32) * flat_size
    scores = scores + jnp.arange(flat_size, dtype=jnp.int32)[None, :]
    order = jnp.argsort(scores, axis=1, stable=True).astype(jnp.int32)
    return order[:, :SLOTS].reshape(REPS, D // CH, LAT // CH, SLOTS)


def strengthened(entries, key, source, target, parts, factor):
    owner, partner = [(jnp.arange(entries.shape[position]) // (entries.shape[position] // parts)).reshape([-1 if axis == position else 1 for axis in range(entries.ndim)]) for position in (source, target)]
    chosen = jax.random.permutation(key, parts)[partner]
    strong = (owner == chosen) | (owner == (partner + parts // 2) % parts)
    return jnp.where(strong, factor * entries, entries)


def shard_levels(own_key, shape, pieces, smallest, largest):
    loudness, own = 1.0, jax.random.fold_in(own_key, 6)
    for dim, blocks in pieces:
        heights = jnp.exp(jax.random.uniform(jax.random.fold_in(own, dim), (blocks,), jnp.float32, smallest / len(pieces), largest / len(pieces)))
        loudness = loudness * jnp.repeat(heights, shape[dim] // blocks).reshape([-1 if axis == dim else 1 for axis in range(len(shape))])
    return loudness


def centred(stream_key, dims, spread, bound, shards=(), kind=jnp.bfloat16):
    values = jax.random.normal(stream_key, dims, jnp.float32) * spread
    if len(shards) > 0:
        values = shard_levels(stream_key, dims, shards, -0.22, 0.18) * values
    return jnp.clip(values, min=-bound, max=bound).astype(kind)


def gaussian_with(rng, dims, spread, reach, pieces, heavy, kind=jnp.bfloat16):
    values = spread * jax.random.normal(rng, dims, jnp.float32)
    if pieces:
        values = values * shard_levels(rng, dims, pieces, -0.22, 0.18)
    return jnp.clip(strengthened(values, jax.random.fold_in(rng, 3), *heavy), -reach, reach).astype(kind)


def setup_inputs(seed: int = 0) -> dict:
    seeds = jax.random.split(jax.random.key(seed), 6)
    return {
        "activations": gaussian_with(seeds[0], (REPS, TOKENS, D), 1.0, 6.0, ((0, 8), (1, 32)), (1, 2, 32, 2.75)),
        "out_grads": centred(seeds[1], (REPS, TOKENS, LAT), TOKENS ** -0.5, 0.0390625, ((0, 8), (1, 32))),
        "momentum": centred(seeds[2], (REPS, D, LAT), 1.0, 6.0, ((0, 8), (1, 32)), jnp.float32),
        "indices": draw_indices(jax.random.fold_in(seeds[5], 71), 0),
        "counts": draw_counts(jax.random.fold_in(seeds[5], 71), 0),
    }


def cosine_table(size):
    freq = lax.broadcasted_iota(jnp.int32, (size, size), 0).astype(jnp.float32)
    place = lax.broadcasted_iota(jnp.int32, (size, size), 1).astype(jnp.float32)
    table = jnp.cos(math.pi * (2.0 * place + 1.0) * freq / (2.0 * size)) * math.sqrt(2.0 / size)
    return jnp.where(freq < 0.5, table * math.sqrt(0.5), table)

def forward_tiles(field, table):
    height, breadth = field.shape
    side = table.shape[0]
    blocks = field.reshape(height // side, side, breadth // side, side)
    result = jnp.einsum('ka,iajb,lb->ijkl', table, blocks, table, precision=lax.Precision.HIGHEST)
    return result.reshape(height // side, breadth // side, side * side)

def inverse_tiles(values, table):
    tile_rows, tile_cols, flat_size = values.shape
    side = table.shape[0]
    grid = values.reshape(tile_rows, tile_cols, side, side)
    blocks = jnp.einsum('ka,ijkl,lb->iajb', table, grid, table, precision=lax.Precision.HIGHEST)
    return blocks.reshape(tile_rows * side, tile_cols * side)

def scatter_slots(values, places, flat_size):
    tile_rows, tile_cols, width_slots = values.shape
    tile_count = tile_rows * tile_cols
    tile_ids = jnp.broadcast_to(jnp.arange(tile_count, dtype=jnp.int32)[:, None], (tile_count, width_slots))
    dense = jnp.zeros((tile_count, flat_size), values.dtype)
    dense = dense.at[tile_ids, places.reshape(tile_count, width_slots).astype(jnp.int32)].add(values.reshape(tile_count, width_slots))
    return dense.reshape(tile_rows, tile_cols, flat_size)

def reference(activations, out_grads, momentum, indices, counts):
    table = cosine_table(CH)

    def one_replica(items):
        inputs, grads, moment_old, places, count = items
        gradient = jnp.einsum('td,tc->dc', inputs.astype(jnp.float32), grads.astype(jnp.float32), precision=lax.Precision.HIGHEST)
        moment = 0.9 * moment_old + gradient
        coefficients = forward_tiles(moment, table)
        picked = jnp.take_along_axis(coefficients, places, axis=2)
        live = jnp.arange(SLOTS, dtype=jnp.int32) < count
        picked = jnp.where(live, picked, jnp.zeros_like(picked))
        sparse = scatter_slots(picked, places, CH * CH)
        return (moment - inverse_tiles(sparse, table), sparse)
    new_momentum, sparse = lax.map(one_replica, (activations, out_grads, momentum, indices, counts))
    total = lax.optimization_barrier(jnp.sum(sparse, axis=0))
    decoded = inverse_tiles(total, table)
    step_dir = decoded * lax.rsqrt(decoded * decoded + 0.04)
    return (new_momentum, step_dir)
```

```python
import math

import jax
import jax.numpy as jnp
import numpy as np
from jax import lax
from jax.experimental import pallas as pl
from jax.experimental.pallas import tpu as pltpu
from jax.sharding import PartitionSpec as P

CH = 64
SLOTS = 128
BF = jnp.bfloat16
F32 = jnp.float32


def cosine_table(side):
    freq = np.arange(side, dtype=np.float64)[:, None]
    place = np.arange(side, dtype=np.float64)[None, :]
    table = np.cos(math.pi * (2.0 * place + 1.0) * freq / (2.0 * side)) * math.sqrt(2.0 / side)
    return np.where(freq < 0.5, table * math.sqrt(0.5), table)


def two_terms(matrix):
    high = matrix.astype(np.float32).astype(BF)
    low = (matrix - high.astype(np.float64)).astype(np.float32).astype(BF)
    return np.stack([high, low])


def split(x):
    high = x.astype(BF)
    return high, (x - high.astype(F32)).astype(BF)


def dot(a, b):
    return jnp.dot(a, b, preferred_element_type=F32)


def dot_nt(a, b):
    return lax.dot_general(a, b, (((1,), (1,)), ((), ())), preferred_element_type=F32)


def left_product(table, x):
    high, low = split(x)
    return dot(table[0], high) + (dot(table[0], low) + dot(table[1], high))


def right_product(x, table):
    width = table.shape[-1]
    pieces = []
    for start in range(0, x.shape[1], width):
        high, low = split(x[:, start:start + width])
        pieces.append(dot(high, table[0]) + (dot(low, table[0]) + dot(high, table[1])))
    return jnp.concatenate(pieces, axis=1)


def pick_kernel(grad, momentum, places, rows, rows_t, cols, cols_t, new_moment, payload, coef, sparse):
    moment = 0.9 * momentum[...] + grad[...]
    coef[...] = right_product(left_product(rows, moment), cols_t)
    tile_rows, tile_cols = grad.shape[0] // CH, grad.shape[1] // CH
    group = 4
    tiles = tile_rows * tile_cols
    for i in range(tile_rows):
        for h in range(tile_cols // group):
            first = i * tile_cols + h * group
            part = [places[first + n:first + n + 1, :] for n in range(group)]
            flat = jnp.concatenate(part, axis=1)
            row_code = flat >> 6
            col_code = jnp.concatenate([(p & 63) + CH * n for n, p in enumerate(part)], axis=1)
            width = group * SLOTS
            in_col = lax.broadcasted_iota(jnp.int32, (group * CH, width), 0) == col_code
            in_row = lax.broadcasted_iota(jnp.int32, (CH, width), 0) == row_code
            col_hot = jnp.where(in_col, 1.0, 0.0).astype(BF)
            row_hot = jnp.where(in_row, 1.0, 0.0).astype(BF)
            block = coef[i * CH:(i + 1) * CH, h * group * CH:(h + 1) * group * CH]
            high, low = split(block)
            spread = dot(high, col_hot) + dot(low, col_hot)
            value = jnp.sum(jnp.where(in_row, spread, 0.0), axis=0, keepdims=True)
            for n in range(group):
                one = value[:, n * SLOTS:(n + 1) * SLOTS]
                for r in range(payload.shape[0]):
                    payload[r, first + n:first + n + 1, :] = one
            sparse[i * CH:(i + 1) * CH, h * group * CH:(h + 1) * group * CH] = block * dot_nt(row_hot, col_hot)
    for r in range(payload.shape[0]):
        payload[r, tiles:, :] = places[...].astype(F32)
    new_moment[...] = moment - right_product(left_product(rows_t, sparse[...]), cols)


def decode_kernel(gathered, rows_t, cols, step_dir, total):
    reps = gathered.shape[0]
    tiles = gathered.shape[1] // 2
    tile_cols = total.shape[1] // CH
    for pair in range(tiles // 2):
        blocks = []
        for t in (2 * pair, 2 * pair + 1):
            highs, lows, hots = [], [], []
            for r in range(reps):
                value = gathered[r, t:t + 1, :]
                place = gathered[r, tiles + t:tiles + t + 1, :].astype(jnp.int32)
                in_row = lax.broadcasted_iota(jnp.int32, (CH, SLOTS), 0) == (place >> 6)
                in_col = lax.broadcasted_iota(jnp.int32, (CH, SLOTS), 0) == (place & 63)
                high, low = split(value)
                highs.append(jnp.where(in_row, high.astype(F32), 0.0).astype(BF))
                lows.append(jnp.where(in_row, low.astype(F32), 0.0).astype(BF))
                hots.append(jnp.where(in_col, 1.0, 0.0).astype(BF))
            both = jnp.concatenate([jnp.concatenate(highs, axis=1), jnp.concatenate(lows, axis=1)], axis=0)
            out = dot_nt(both, jnp.concatenate(hots, axis=1))
            blocks.append(out[:CH] + out[CH:])
        i, j = (2 * pair) // tile_cols, (2 * pair) % tile_cols
        total[i * CH:(i + 1) * CH, j * CH:(j + 2) * CH] = jnp.concatenate(blocks, axis=1)
    decoded = right_product(left_product(rows_t, total[...]), cols)
    step_dir[...] = decoded * lax.rsqrt(decoded * decoded + 0.04)


def body(activations, out_grads, momentum, indices, counts):
    reps = lax.axis_size("rep")
    table = cosine_table(CH)
    rows = np.kron(np.eye(3), table)
    cols = np.kron(np.eye(4), table)
    rows, rows_t, cols, cols_t = (jnp.asarray(two_terms(m)) for m in (rows, rows.T, cols, cols.T))
    height, breadth = momentum.shape[1:]
    tiles = (height // CH) * (breadth // CH)
    live = lax.broadcasted_iota(jnp.int32, indices.shape[1:], 2) < counts[0]
    places = jnp.where(live, indices[0], -1).reshape(tiles, SLOTS)
    gradient = lax.psum_scatter(
        lax.dot_general(activations[0], out_grads[0], (((0,), (0,)), ((), ())), preferred_element_type=F32),
        "fsdp", scatter_dimension=0, tiled=True,
    )
    new_moment, payload = pl.pallas_call(
        pick_kernel,
        out_shape=[
            jax.ShapeDtypeStruct((height, breadth), F32),
            jax.ShapeDtypeStruct((reps, 2 * tiles, SLOTS), F32),
        ],
        scratch_shapes=[pltpu.VMEM((height, breadth), F32), pltpu.VMEM((height, breadth), F32)],
        compiler_params=pltpu.CompilerParams(vmem_limit_bytes=32 << 20),
        name="pick",
    )(gradient, momentum[0], places, rows, rows_t, cols, cols_t)
    gathered = lax.all_to_all(payload, "rep", 0, 0)
    step_dir = pl.pallas_call(
        decode_kernel,
        out_shape=jax.ShapeDtypeStruct((height, breadth), F32),
        scratch_shapes=[pltpu.VMEM((height, breadth), F32)],
        compiler_params=pltpu.CompilerParams(vmem_limit_bytes=32 << 20),
        name="decode",
    )(gathered, rows_t, cols)
    return (new_moment[None], step_dir)


def solution(mesh):
    placed = (
        P("rep", "fsdp", None),
        P("rep", "fsdp", None),
        P("rep", "fsdp", None),
        P("rep", "fsdp", None, None),
        P("rep"),
    )
    return jax.shard_map(
        body,
        mesh=mesh,
        in_specs=placed,
        out_specs=(P("rep", "fsdp", None), P("fsdp", None)),
        check_vma=False,
    )
```

```python
import math

import jax
import jax.numpy as jnp
import numpy as np
from jax import lax
from jax.experimental import pallas as pl
from jax.experimental.pallas import tpu as pltpu
from jax.sharding import PartitionSpec as P

CH = 64
SLOTS = 128
BF = jnp.bfloat16
F32 = jnp.float32
I16 = jnp.int16
HEAD = 16
ORDER = (4, 3, -3, 2, -2, 1, -1, 0)
VMEM = 40 << 20


def cosine_table(side):
    freq = np.arange(side, dtype=np.float64)[:, None]
    place = np.arange(side, dtype=np.float64)[None, :]
    table = np.cos(math.pi * (2.0 * place + 1.0) * freq / (2.0 * side)) * math.sqrt(2.0 / side)
    return np.where(freq < 0.5, table * math.sqrt(0.5), table)


def two_terms(matrix):
    high = matrix.astype(np.float32).astype(BF)
    low = (matrix - high.astype(np.float64)).astype(np.float32).astype(BF)
    return np.stack([high, low])


def split(x):
    high = x.astype(BF)
    return high, (x - high.astype(F32)).astype(BF)


def dot(a, b):
    return jnp.dot(a, b, preferred_element_type=F32)


def dot_nt(a, b):
    return lax.dot_general(a, b, (((1,), (1,)), ((), ())), preferred_element_type=F32)


def left_product(table, x):
    high, low = split(x)
    return dot(table[0], high) + (dot(table[0], low) + dot(table[1], high))


def right_product(x, table):
    width = table.shape[-1]
    pieces = []
    for start in range(0, x.shape[1], width):
        high, low = split(x[:, start:start + width])
        pieces.append(dot(high, table[0]) + (dot(low, table[0]) + dot(high, table[1])))
    return jnp.concatenate(pieces, axis=1)


def encode(x, out):
    top = jnp.max(jnp.abs(x), axis=0, keepdims=True)
    code = jnp.ceil(128.0 * jnp.log2(jnp.maximum(top, 1e-30))) + 1.0
    scale = 32767.0 * jnp.exp2(code * (-1.0 / 128.0))
    height = x.shape[0]
    out[:height, :] = jnp.round(x * scale).astype(jnp.int32).astype(I16)
    out[height:, :] = jnp.broadcast_to(code, (HEAD, x.shape[1])).astype(jnp.int32).astype(I16)


def decode(ref):
    height = ref.shape[0] - HEAD
    code = ref[height:, :].astype(jnp.int32).astype(F32)[:1, :]
    scale = jnp.exp2(code * (1.0 / 128.0)) * (1.0 / 32767.0)
    return ref[:height, :].astype(jnp.int32).astype(F32) * scale


def product_kernel(spot, inputs, grads, away, kept, both):
    both[...] = lax.dot_general(inputs[...], grads[...], (((0,), (0,)), ((), ())), preferred_element_type=F32)
    height = kept.shape[0]
    core = spot[spot.shape[0] - 1]
    kept[...] = both[pl.ds(pl.multiple_of(core * height, height), height), :]
    encode(both[pl.ds(pl.multiple_of((1 - core) * height, height), height), :], away)


def products(inputs, grads, blocks, core, height):
    tokens, breadth = grads.shape
    steps = blocks.shape[0]
    return pl.pallas_call(
        product_kernel,
        grid_spec=pltpu.PrefetchScalarGridSpec(
            num_scalar_prefetch=1,
            grid=(steps,),
            in_specs=[
                pl.BlockSpec((tokens, 2 * height), lambda i, spot: (0, spot[i])),
                pl.BlockSpec((tokens, breadth), lambda i, spot: (0, 0)),
            ],
            out_specs=[
                pl.BlockSpec((None, height + HEAD, breadth), lambda i, spot: (i, 0, 0)),
                pl.BlockSpec((None, height, breadth), lambda i, spot: (i, 0, 0)),
            ],
            scratch_shapes=[pltpu.VMEM((2 * height, breadth), F32)],
        ),
        out_shape=[
            jax.ShapeDtypeStruct((steps, height + HEAD, breadth), I16),
            jax.ShapeDtypeStruct((steps, height, breadth), F32),
        ],
        compiler_params=pltpu.CompilerParams(vmem_limit_bytes=VMEM),
        cost_estimate=pl.CostEstimate(
            flops=steps * 4 * height * tokens * breadth,
            bytes_accessed=steps * (4 * height * tokens + 6 * height * breadth),
            transcendentals=0,
        ),
        name="products",
    )(jnp.concatenate([blocks, core[None]]), inputs, grads)


def hop_kernel(columns, *refs):
    kept, other = refs[:2]
    out = refs[-1]
    total = kept[...] + decode(other)
    for ref in refs[2:-1]:
        part = decode(ref)
        if part.shape[1] < total.shape[1]:
            pad = jnp.zeros((part.shape[0], total.shape[1] - part.shape[1]), F32)
            part = jnp.concatenate([pad, part] if columns else [part, pad], axis=1)
        total = total + part
    if out.shape[1] < total.shape[1]:
        width = out.shape[1]
        total = total[:, columns * width:(columns + 1) * width]
    encode(total, out)


def hop(kept, other, slot, arrived, columns, width):
    steps, height, breadth = kept.shape
    return pl.pallas_call(
        lambda *refs: hop_kernel(columns, *refs),
        grid=(1,),
        in_specs=[
            pl.BlockSpec((None, height, breadth), lambda i: (slot, 0, 0)),
            pl.BlockSpec((None, height + HEAD, breadth), lambda i: (slot, 0, 0)),
        ] + [pl.BlockSpec(a.shape, lambda i: (0, 0)) for a in arrived],
        out_specs=pl.BlockSpec((height + HEAD, width), lambda i: (0, 0)),
        out_shape=jax.ShapeDtypeStruct((height + HEAD, width), I16),
        compiler_params=pltpu.CompilerParams(vmem_limit_bytes=VMEM),
        cost_estimate=pl.CostEstimate(flops=10 * height * breadth, bytes_accessed=10 * height * breadth, transcendentals=0),
        name="hop",
    )(kept, other, *arrived)


def ring_sum(kept, other, ahead, behind):
    def at(slot):
        for (start, array), (_, remote) in zip(reversed(kept), reversed(other)):
            if slot >= start:
                return array, remote, slot - start

    breadth = kept[0][1].shape[2]
    half = breadth // 2
    forth = lax.ppermute(hop(*at(0), [], 0, half), "fsdp", ahead)
    back = lax.ppermute(hop(*at(0), [], 1, half), "fsdp", behind)
    for step in range(3):
        forth = lax.ppermute(hop(*at(1 + 2 * step), [forth], 0, breadth), "fsdp", ahead)
        back = lax.ppermute(hop(*at(2 + 2 * step), [back], 1, breadth), "fsdp", behind)
    return (*at(7), [forth, back])


def pick_kernel(kept, other, forth, back, across, momentum, places, rows, rows_t, cols, cols_t, new_moment, payload, coef, sparse):
    grad = kept[...] + decode(other) + decode(forth) + decode(back) + decode(across)
    moment = 0.9 * momentum[...] + grad
    coef[...] = right_product(left_product(rows, moment), cols_t)
    tile_rows, tile_cols = grad.shape[0] // CH, grad.shape[1] // CH
    group = 4
    tiles = tile_rows * tile_cols
    for i in range(tile_rows):
        for h in range(tile_cols // group):
            first = i * tile_cols + h * group
            part = [places[first + n:first + n + 1, :] for n in range(group)]
            flat = jnp.concatenate(part, axis=1)
            row_code = flat >> 6
            col_code = jnp.concatenate([(p & 63) + CH * n for n, p in enumerate(part)], axis=1)
            width = group * SLOTS
            in_col = lax.broadcasted_iota(jnp.int32, (group * CH, width), 0) == col_code
            in_row = lax.broadcasted_iota(jnp.int32, (CH, width), 0) == row_code
            col_hot = jnp.where(in_col, 1.0, 0.0).astype(BF)
            row_hot = jnp.where(in_row, 1.0, 0.0).astype(BF)
            block = coef[i * CH:(i + 1) * CH, h * group * CH:(h + 1) * group * CH]
            high, low = split(block)
            spread = dot(high, col_hot) + dot(low, col_hot)
            value = jnp.sum(jnp.where(in_row, spread, 0.0), axis=0, keepdims=True)
            for n in range(group):
                one = value[:, n * SLOTS:(n + 1) * SLOTS]
                for r in range(payload.shape[0]):
                    payload[r, first + n:first + n + 1, :] = one
            sparse[i * CH:(i + 1) * CH, h * group * CH:(h + 1) * group * CH] = block * dot_nt(row_hot, col_hot)
    for r in range(payload.shape[0]):
        payload[r, tiles:, :] = places[...].astype(F32)
    new_moment[...] = moment - right_product(left_product(rows_t, sparse[...]), cols)


def decode_kernel(gathered, rows_t, cols, step_dir, total):
    reps = gathered.shape[0]
    tiles = gathered.shape[1] // 2
    tile_cols = total.shape[1] // CH
    for pair in range(tiles // 2):
        blocks = []
        for t in (2 * pair, 2 * pair + 1):
            highs, lows, hots = [], [], []
            for r in range(reps):
                value = gathered[r, t:t + 1, :]
                place = gathered[r, tiles + t:tiles + t + 1, :].astype(jnp.int32)
                in_row = lax.broadcasted_iota(jnp.int32, (CH, SLOTS), 0) == (place >> 6)
                in_col = lax.broadcasted_iota(jnp.int32, (CH, SLOTS), 0) == (place & 63)
                high, low = split(value)
                highs.append(jnp.where(in_row, high.astype(F32), 0.0).astype(BF))
                lows.append(jnp.where(in_row, low.astype(F32), 0.0).astype(BF))
                hots.append(jnp.where(in_col, 1.0, 0.0).astype(BF))
            both = jnp.concatenate([jnp.concatenate(highs, axis=1), jnp.concatenate(lows, axis=1)], axis=0)
            out = dot_nt(both, jnp.concatenate(hots, axis=1))
            blocks.append(out[:CH] + out[CH:])
        i, j = (2 * pair) // tile_cols, (2 * pair) % tile_cols
        total[i * CH:(i + 1) * CH, j * CH:(j + 2) * CH] = jnp.concatenate(blocks, axis=1)
    decoded = right_product(left_product(rows_t, total[...]), cols)
    step_dir[...] = decoded * lax.rsqrt(decoded * decoded + 0.04)


def body(activations, out_grads, momentum, indices, counts):
    reps = lax.axis_size("rep")
    table = cosine_table(CH)
    rows = np.kron(np.eye(3), table)
    cols = np.kron(np.eye(4), table)
    rows, rows_t, cols, cols_t = (jnp.asarray(two_terms(m)) for m in (rows, rows.T, cols, cols.T))
    height, breadth = momentum.shape[1:]
    tiles = (height // CH) * (breadth // CH)
    live = lax.broadcasted_iota(jnp.int32, indices.shape[1:], 2) < counts[0]
    places = jnp.where(live, indices[0], -1).reshape(tiles, SLOTS)
    chips = lax.axis_size("fsdp") // 4
    me = lax.axis_index("fsdp")
    z, y, core = me // 4, (me // 2) % 2, me % 2

    def route(move):
        pairs = []
        for place in range(4 * chips):
            to_z, to_y, to_core = move(place // 4, (place // 2) % 2, place % 2)
            pairs.append((place, ((to_z % chips) * 2 + to_y) * 2 + to_core))
        return pairs

    ahead = route(lambda z, y, c: (z + 1, y, c))
    behind = route(lambda z, y, c: (z - 1, y, c))
    beside = route(lambda z, y, c: (z, 1 - y, c))
    within = route(lambda z, y, c: (z, y, 1 - c))
    order = np.array(ORDER, np.int32)
    inputs, grads = activations[0], out_grads[0]

    def stream(target, cuts):
        blocks = ((z + order) % chips) * 2 + target
        kept, other = [], []
        for start, stop in zip(cuts[:-1], cuts[1:]):
            away, own = products(inputs, grads, blocks[start:stop], core, height)
            kept.append((start, own))
            other.append((start, lax.ppermute(away, "fsdp", within)))
        return kept, other

    first = stream(1 - y, (0, 3, 8))
    second = stream(y, (0, 3, 8))
    part, remote, slot, ends = ring_sum(*first, ahead, behind)
    across = lax.ppermute(hop(part, remote, slot, ends, 0, breadth), "fsdp", beside)
    part, remote, slot, ends = ring_sum(*second, ahead, behind)

    def whole(array):
        return pl.BlockSpec(array.shape, lambda i, n=array.ndim: (0,) * n)

    rest = (*ends, across, momentum[0], places, rows, rows_t, cols, cols_t)
    new_moment, payload = pl.pallas_call(
        pick_kernel,
        grid=(1,),
        in_specs=[
            pl.BlockSpec((None, height, breadth), lambda i: (slot, 0, 0)),
            pl.BlockSpec((None, height + HEAD, breadth), lambda i: (slot, 0, 0)),
        ] + [whole(a) for a in rest],
        out_specs=[
            pl.BlockSpec((height, breadth), lambda i: (0, 0)),
            pl.BlockSpec((reps, 2 * tiles, SLOTS), lambda i: (0, 0, 0)),
        ],
        out_shape=[
            jax.ShapeDtypeStruct((height, breadth), F32),
            jax.ShapeDtypeStruct((reps, 2 * tiles, SLOTS), F32),
        ],
        scratch_shapes=[pltpu.VMEM((height, breadth), F32), pltpu.VMEM((height, breadth), F32)],
        compiler_params=pltpu.CompilerParams(vmem_limit_bytes=VMEM),
        name="pick",
    )(part, remote, *rest)
    gathered = lax.all_to_all(payload, "rep", 0, 0)
    step_dir = pl.pallas_call(
        decode_kernel,
        out_shape=jax.ShapeDtypeStruct((height, breadth), F32),
        scratch_shapes=[pltpu.VMEM((height, breadth), F32)],
        compiler_params=pltpu.CompilerParams(vmem_limit_bytes=32 << 20),
        name="decode",
    )(gathered, rows_t, cols)
    return (new_moment[None], step_dir)


def solution(mesh):
    placed = (
        P("rep", "fsdp", None),
        P("rep", "fsdp", None),
        P("rep", "fsdp", None),
        P("rep", "fsdp", None, None),
        P("rep"),
    )
    return jax.shard_map(
        body,
        mesh=mesh,
        in_specs=placed,
        out_specs=(P("rep", "fsdp", None), P("fsdp", None)),
        check_vma=False,
    )
```

```python
import math

import jax
import jax.numpy as jnp
import numpy as np
from jax import lax
from jax.experimental import pallas as pl
from jax.experimental.pallas import tpu as pltpu
from jax.sharding import PartitionSpec as P

CH = 64
SLOTS = 128
BF = jnp.bfloat16
F32 = jnp.float32
I16 = jnp.int16
HEAD = 16
RINGS = 8
ROWS = 192
BOTH = 2 * ROWS


def cosine_table(side):
    freq = np.arange(side, dtype=np.float64)[:, None]
    place = np.arange(side, dtype=np.float64)[None, :]
    table = np.cos(math.pi * (2.0 * place + 1.0) * freq / (2.0 * side)) * math.sqrt(2.0 / side)
    return np.where(freq < 0.5, table * math.sqrt(0.5), table)


def two_terms(matrix):
    high = matrix.astype(np.float32).astype(BF)
    low = (matrix - high.astype(np.float64)).astype(np.float32).astype(BF)
    return np.stack([high, low])


def split(x):
    high = x.astype(BF)
    return high, (x - high.astype(F32)).astype(BF)


def dot(a, b):
    return jnp.dot(a, b, preferred_element_type=F32)


def dot_nt(a, b):
    return lax.dot_general(a, b, (((1,), (1,)), ((), ())), preferred_element_type=F32)


def left_product(table, x):
    high, low = split(x)
    return dot(table[0], high) + (dot(table[0], low) + dot(table[1], high))


def right_product(x, table):
    width = table.shape[-1]
    pieces = []
    for start in range(0, x.shape[1], width):
        high, low = split(x[:, start:start + width])
        pieces.append(dot(high, table[0]) + (dot(low, table[0]) + dot(high, table[1])))
    return jnp.concatenate(pieces, axis=1)


def encode(x, out):
    top = jnp.max(jnp.abs(x), axis=0, keepdims=True)
    code = jnp.ceil(128.0 * jnp.log2(jnp.maximum(top, 1e-30))) + 1.0
    scale = 32767.0 * jnp.exp2(code * (-1.0 / 128.0))
    height = x.shape[0]
    out[:height, :] = jnp.round(x * scale).astype(jnp.int32).astype(I16)
    out[height:, :] = jnp.broadcast_to(code, (HEAD, x.shape[1])).astype(jnp.int32).astype(I16)


def decode(ref):
    height = ref.shape[0] - HEAD
    code = ref[height:, :].astype(jnp.int32).astype(F32)[:1, :]
    scale = jnp.exp2(code * (1.0 / 128.0)) * (1.0 / 32767.0)
    return ref[:height, :].astype(jnp.int32).astype(F32) * scale


def place():
    me = lax.axis_index("fsdp")
    return me // 4, lax.rem(me // 2, 2), lax.rem(me, 2)


def route(move):
    pairs = []
    for source in range(4 * RINGS):
        z, y, core = move(source // 4, (source // 2) % 2, source % 2)
        pairs.append((source, ((z % RINGS) * 2 + y) * 2 + core))
    return pairs


ALONG = route(lambda z, y, c: (z + 1 - 2 * c, y, c))
ASLANT = route(lambda z, y, c: (z + 1 - 2 * c, 1 - y, c))
BESIDE = route(lambda z, y, c: (z, 1 - y, c))
WITHIN = route(lambda z, y, c: (z, y, 1 - c))


def product(left, right):
    return lax.dot_general(left, right, (((0,), (0,)), ((), ())), preferred_element_type=F32)


def load_blocks(steps, swap, inputs, grads, blocks, whole, sems):
    z, y, core = place()
    target = 1 - y if swap else y
    copies = [pltpu.make_async_copy(grads, whole, sems.at[len(steps)])]
    for n, step in enumerate(steps):
        block = lax.rem(z + step * (1 - 2 * core) + RINGS, RINGS) * 2 + target
        columns = pl.ds(pl.multiple_of(block * BOTH, BOTH), BOTH)
        copies.append(pltpu.make_async_copy(inputs.at[:, columns], blocks.at[n], sems.at[n]))
    for copy in copies:
        copy.start()
    copies[0].wait()
    return core, copies[1:]


AWAY = (4, -3, -2, -1, 0)
KEPT = (3, 2, 1)


def away_kernel(swap, inputs, grads, _, keep4, keep0, away, blocks, whole, both, sems):
    core, copies = load_blocks(AWAY, swap, inputs, grads, blocks, whole, sems)
    half = keep4.shape[1]
    copies[0].wait()
    both[...] = product(blocks[0], whole[...])
    keep4[...] = both[:, pl.ds(pl.multiple_of(core * half, half), half)]
    other = both[:, pl.ds(pl.multiple_of((1 - core) * half, half), half)]
    encode(other[:ROWS], away.at[0, :, :half])
    encode(other[ROWS:], away.at[0, :, half:])
    for n in (1, 2, 3):
        copies[n].wait()
        total = product(blocks[n], whole[...])
        encode(total[:ROWS], away.at[2 * n - 1])
        encode(total[ROWS:], away.at[2 * n])
    copies[4].wait()
    both[...] = product(blocks[4], whole[...])
    keep0[...] = both[pl.ds(pl.multiple_of(core * ROWS, ROWS), ROWS), :]
    encode(both[pl.ds(pl.multiple_of((1 - core) * ROWS, ROWS), ROWS), :], away.at[7])


def kept_kernel(swap, inputs, grads, _, keep3, keep2, keep1, blocks, whole, sems):
    _, copies = load_blocks(KEPT, swap, inputs, grads, blocks, whole, sems)
    for n, keep in enumerate((keep3, keep2, keep1)):
        copies[n].wait()
        keep[...] = product(blocks[n], whole[...])


def partial_sums(kernel, swap, inputs, grads, after, steps, outs, scratch, name):
    tokens, breadth = grads.shape
    return pl.pallas_call(
        lambda *refs: kernel(swap, *refs),
        in_specs=[pl.BlockSpec(memory_space=pl.ANY)] * 3,
        out_shape=[jax.ShapeDtypeStruct(*out) for out in outs],
        scratch_shapes=[
            pltpu.VMEM((steps, tokens, BOTH), BF),
            pltpu.VMEM((tokens, breadth), BF),
            *scratch,
            pltpu.SemaphoreType.DMA((steps + 1,)),
        ],
        compiler_params=pltpu.CompilerParams(vmem_limit_bytes=56 << 20),
        cost_estimate=pl.CostEstimate(
            flops=steps * 6 * BOTH * tokens * breadth,
            bytes_accessed=steps * (2 * BOTH * tokens + 2 * BOTH * breadth),
            transcendentals=0,
        ),
        name=name,
    )(inputs, grads, after)


def away_sums(swap, inputs, grads, after):
    breadth = grads.shape[1]
    outs = [((BOTH, breadth // 2), F32), ((ROWS, breadth), F32), ((8, ROWS + HEAD, breadth), I16)]
    return partial_sums(away_kernel, swap, inputs, grads, after, len(AWAY), outs, [pltpu.VMEM((BOTH, breadth), F32)], "away")


def kept_sums(swap, inputs, grads, after):
    outs = [((BOTH, grads.shape[1]), F32)] * 3
    return partial_sums(kept_kernel, swap, inputs, grads, after, len(KEPT), outs, [], "kept")


ANYWHERE = "any"


def call_local(kernel, args, specs, outs, name, scratch=()):
    def spec(arg, cut):
        if cut == ANYWHERE:
            return pl.BlockSpec(memory_space=pl.ANY)
        block, index = cut or (arg.shape, (0,) * arg.ndim)
        return pl.BlockSpec(block, lambda i: index)

    result = pl.pallas_call(
        kernel,
        grid=(1,),
        in_specs=[spec(arg, cut) for arg, cut in zip(args, specs)],
        out_specs=[pl.BlockSpec(shape, lambda i, n=len(shape): (0,) * n) for shape, _ in outs],
        out_shape=[jax.ShapeDtypeStruct(*out) for out in outs],
        scratch_shapes=list(scratch),
        compiler_params=pltpu.CompilerParams(vmem_limit_bytes=16 << 20),
        cost_estimate=pl.CostEstimate(flops=10 * BOTH * 512, bytes_accessed=10 * BOTH * 512, transcendentals=0),
        name=name,
    )(*args)
    return result


def decode_pair(low, high):
    return jnp.concatenate([decode(low), decode(high)], axis=0)


def first_hop_kernel(keep, other, out):
    half = keep.shape[1]
    encode(keep[...] + decode_pair(other.at[:, :half], other.at[:, half:]), out)


def second_hop_kernel(keep, low, high, arrived, _, out, total):
    half = arrived.shape[1]
    total[...] = keep[...] + decode_pair(low, high)
    mine = pl.ds(pl.multiple_of(place()[2] * half, half), half)
    total[:, mine] += decode(arrived)
    encode(total[...], out)


def later_hop_kernel(keep, low, high, arrived, *rest):
    out = rest[-1]
    encode(keep[...] + decode_pair(low, high) + decode(arrived), out)


def own_kernel(keep, other, out):
    encode(keep[...] + decode(other), out)


def meet_kernel(straight, aslant, keep, other, beside, kept, away, total):
    core = place()[2]
    total[...] = decode(straight) + decode(aslant)
    kept[...] = total[pl.ds(pl.multiple_of(core * ROWS, ROWS), ROWS), :] + keep[...] + decode(other) + decode(beside)
    encode(total[pl.ds(pl.multiple_of((1 - core) * ROWS, ROWS), ROWS), :], away)


def replica_sum(inputs, grads):
    breadth = grads.shape[1]
    tall, short = BOTH + HEAD, ROWS + HEAD

    def send(array, pairs):
        return lax.ppermute(array, "fsdp", pairs)

    def unit(n):
        return (None, short, breadth), (n, 0, 0)

    def first_hop(keep, other):
        return call_local(first_hop_kernel, (keep, other), (None, unit(0)), [((tall, breadth // 2), I16)], "hop1")[0]

    def later_hop(step, keep, other, arrived, after):
        first = 2 * step - 3
        scratch = [pltpu.VMEM((BOTH, breadth), F32)] if step == 2 else []
        return call_local(
            second_hop_kernel if step == 2 else later_hop_kernel,
            (keep, other, other, arrived, after), (None, unit(first), unit(first + 1), None, ANYWHERE),
            [((tall, breadth), I16)], "hop%d" % step, scratch)[0]

    keep4_a, keep0_a, away = away_sums(True, inputs, grads, inputs)
    other_a = send(away, WITHIN)
    keep4_b, keep0_b, away = away_sums(False, inputs, grads, away)
    other_b = send(away, WITHIN)
    ring_a = first_hop(keep4_a, other_a)
    ring_b = first_hop(keep4_b, other_b)
    kept_a = kept_sums(True, inputs, grads, ring_a)
    kept_b = kept_sums(False, inputs, grads, ring_b)
    own_a = call_local(own_kernel, (keep0_a, other_a), (None, unit(7)), [((short, breadth), I16)], "own")[0]
    beside = send(own_a, BESIDE)
    for step in (2, 3, 4):
        ring_a = later_hop(step, kept_a[step - 2], other_a, send(ring_a, ALONG), own_a)
        ring_b = later_hop(step, kept_b[step - 2], other_b, send(ring_b, ALONG), own_a)
    ring_a, ring_b = send(ring_a, ASLANT), send(ring_b, ALONG)
    kept, away = call_local(
        meet_kernel, (ring_b, ring_a, keep0_b, other_b, beside), (None, None, None, unit(7), None),
        [((ROWS, breadth), F32), ((short, breadth), I16)], "meet", [pltpu.VMEM((BOTH, breadth), F32)])
    return kept, send(away, WITHIN)


def pick_kernel(kept, other, momentum, places, rows, rows_t, cols, cols_t, new_moment, payload, coef, sparse):
    grad = kept[...] + decode(other)
    moment = 0.9 * momentum[...] + grad
    coef[...] = right_product(left_product(rows, moment), cols_t)
    tile_rows, tile_cols = grad.shape[0] // CH, grad.shape[1] // CH
    group = 4
    tiles = tile_rows * tile_cols
    for i in range(tile_rows):
        for h in range(tile_cols // group):
            first = i * tile_cols + h * group
            part = [places[first + n:first + n + 1, :] for n in range(group)]
            flat = jnp.concatenate(part, axis=1)
            row_code = flat >> 6
            col_code = jnp.concatenate([(p & 63) + CH * n for n, p in enumerate(part)], axis=1)
            width = group * SLOTS
            in_col = lax.broadcasted_iota(jnp.int32, (group * CH, width), 0) == col_code
            in_row = lax.broadcasted_iota(jnp.int32, (CH, width), 0) == row_code
            col_hot = jnp.where(in_col, 1.0, 0.0).astype(BF)
            row_hot = jnp.where(in_row, 1.0, 0.0).astype(BF)
            block = coef[i * CH:(i + 1) * CH, h * group * CH:(h + 1) * group * CH]
            high, low = split(block)
            spread = dot(high, col_hot) + dot(low, col_hot)
            value = jnp.sum(jnp.where(in_row, spread, 0.0), axis=0, keepdims=True)
            for n in range(group):
                one = value[:, n * SLOTS:(n + 1) * SLOTS]
                for r in range(payload.shape[0]):
                    payload[r, first + n:first + n + 1, :] = one
            sparse[i * CH:(i + 1) * CH, h * group * CH:(h + 1) * group * CH] = block * dot_nt(row_hot, col_hot)
    for r in range(payload.shape[0]):
        payload[r, tiles:, :] = places[...].astype(F32)
    new_moment[...] = moment - right_product(left_product(rows_t, sparse[...]), cols)


def decode_kernel(gathered, rows_t, cols, step_dir, total):
    reps = gathered.shape[0]
    tiles = gathered.shape[1] // 2
    tile_cols = total.shape[1] // CH
    for pair in range(tiles // 2):
        blocks = []
        for t in (2 * pair, 2 * pair + 1):
            highs, lows, hots = [], [], []
            for r in range(reps):
                value = gathered[r, t:t + 1, :]
                place = gathered[r, tiles + t:tiles + t + 1, :].astype(jnp.int32)
                in_row = lax.broadcasted_iota(jnp.int32, (CH, SLOTS), 0) == (place >> 6)
                in_col = lax.broadcasted_iota(jnp.int32, (CH, SLOTS), 0) == (place & 63)
                high, low = split(value)
                highs.append(jnp.where(in_row, high.astype(F32), 0.0).astype(BF))
                lows.append(jnp.where(in_row, low.astype(F32), 0.0).astype(BF))
                hots.append(jnp.where(in_col, 1.0, 0.0).astype(BF))
            both = jnp.concatenate([jnp.concatenate(highs, axis=1), jnp.concatenate(lows, axis=1)], axis=0)
            out = dot_nt(both, jnp.concatenate(hots, axis=1))
            blocks.append(out[:CH] + out[CH:])
        i, j = (2 * pair) // tile_cols, (2 * pair) % tile_cols
        total[i * CH:(i + 1) * CH, j * CH:(j + 2) * CH] = jnp.concatenate(blocks, axis=1)
    decoded = right_product(left_product(rows_t, total[...]), cols)
    step_dir[...] = decoded * lax.rsqrt(decoded * decoded + 0.04)


def body(activations, out_grads, momentum, indices, counts):
    reps = lax.axis_size("rep")
    table = cosine_table(CH)
    rows = np.kron(np.eye(3), table)
    cols = np.kron(np.eye(4), table)
    rows, rows_t, cols, cols_t = (jnp.asarray(two_terms(m)) for m in (rows, rows.T, cols, cols.T))
    height, breadth = momentum.shape[1:]
    tiles = (height // CH) * (breadth // CH)
    live = lax.broadcasted_iota(jnp.int32, indices.shape[1:], 2) < counts[0]
    places = jnp.where(live, indices[0], -1).reshape(tiles, SLOTS)
    kept, other = replica_sum(activations[0], out_grads[0])
    new_moment, payload = pl.pallas_call(
        pick_kernel,
        out_shape=[
            jax.ShapeDtypeStruct((height, breadth), F32),
            jax.ShapeDtypeStruct((reps, 2 * tiles, SLOTS), F32),
        ],
        scratch_shapes=[pltpu.VMEM((height, breadth), F32), pltpu.VMEM((height, breadth), F32)],
        compiler_params=pltpu.CompilerParams(vmem_limit_bytes=32 << 20),
        name="pick",
    )(kept, other, momentum[0], places, rows, rows_t, cols, cols_t)
    gathered = lax.all_to_all(payload, "rep", 0, 0)
    step_dir = pl.pallas_call(
        decode_kernel,
        out_shape=jax.ShapeDtypeStruct((height, breadth), F32),
        scratch_shapes=[pltpu.VMEM((height, breadth), F32)],
        compiler_params=pltpu.CompilerParams(vmem_limit_bytes=32 << 20),
        name="decode",
    )(gathered, rows_t, cols)
    return (new_moment[None], step_dir)


def solution(mesh):
    placed = (
        P("rep", "fsdp", None),
        P("rep", "fsdp", None),
        P("rep", "fsdp", None),
        P("rep", "fsdp", None, None),
        P("rep"),
    )
    return jax.shard_map(
        body,
        mesh=mesh,
        in_specs=placed,
        out_specs=(P("rep", "fsdp", None), P("fsdp", None)),
        check_vma=False,
    )
```

```python
import math

import jax
import jax.numpy as jnp
import numpy as np
from jax import lax
from jax.experimental import pallas as pl
from jax.experimental.pallas import tpu as pltpu
from jax.sharding import PartitionSpec as P

CH = 64
SLOTS = 128
BF = jnp.bfloat16
F32 = jnp.float32
I16 = jnp.int16
HEAD = 16
RINGS = 8
ROWS = 192
BOTH = 2 * ROWS


def cosine_table(side):
    freq = np.arange(side, dtype=np.float64)[:, None]
    place = np.arange(side, dtype=np.float64)[None, :]
    table = np.cos(math.pi * (2.0 * place + 1.0) * freq / (2.0 * side)) * math.sqrt(2.0 / side)
    return np.where(freq < 0.5, table * math.sqrt(0.5), table)


def two_terms(matrix):
    high = matrix.astype(np.float32).astype(BF)
    low = (matrix - high.astype(np.float64)).astype(np.float32).astype(BF)
    return np.stack([high, low])


def split(x):
    high = x.astype(BF)
    return high, (x - high.astype(F32)).astype(BF)


def dot(a, b):
    return jnp.dot(a, b, preferred_element_type=F32)


def dot_nt(a, b):
    return lax.dot_general(a, b, (((1,), (1,)), ((), ())), preferred_element_type=F32)


def left_product(table, x):
    high, low = split(x)
    return dot(table[0], high) + (dot(table[0], low) + dot(table[1], high))


def right_product(x, table):
    width = table.shape[-1]
    pieces = []
    for start in range(0, x.shape[1], width):
        high, low = split(x[:, start:start + width])
        pieces.append(dot(high, table[0]) + (dot(low, table[0]) + dot(high, table[1])))
    return jnp.concatenate(pieces, axis=1)


def encode(x, out):
    top = jnp.max(jnp.abs(x), axis=0, keepdims=True)
    code = jnp.ceil(128.0 * jnp.log2(jnp.maximum(top, 1e-30))) + 1.0
    scale = 32767.0 * jnp.exp2(code * (-1.0 / 128.0))
    height = x.shape[0]
    out[:height, :] = jnp.round(x * scale).astype(jnp.int32).astype(I16)
    out[height:, :] = jnp.broadcast_to(code, (HEAD, x.shape[1])).astype(jnp.int32).astype(I16)


def decode(ref):
    height = ref.shape[0] - HEAD
    code = ref[height:, :].astype(jnp.int32).astype(F32)[:1, :]
    scale = jnp.exp2(code * (1.0 / 128.0)) * (1.0 / 32767.0)
    return ref[:height, :].astype(jnp.int32).astype(F32) * scale


def place():
    me = lax.axis_index("fsdp")
    return me // 4, lax.rem(me // 2, 2), lax.rem(me, 2)


def route(move):
    pairs = []
    for source in range(4 * RINGS):
        z, y, core = move(source // 4, (source // 2) % 2, source % 2)
        pairs.append((source, ((z % RINGS) * 2 + y) * 2 + core))
    return pairs


ALONG = route(lambda z, y, c: (z + 1 - 2 * c, y, c))
ASLANT = route(lambda z, y, c: (z + 1 - 2 * c, 1 - y, c))
BESIDE = route(lambda z, y, c: (z, 1 - y, c))
WITHIN = route(lambda z, y, c: (z, y, 1 - c))


def product(left, right):
    return lax.dot_general(left, right, (((0,), (0,)), ((), ())), preferred_element_type=F32)


def blocks_in_turn(steps, swap, inputs, grads, blocks, whole, sems):
    z, y, core = place()
    target = 1 - y if swap else y

    def load(n):
        block = lax.rem(z + steps[n] * (1 - 2 * core) + RINGS, RINGS) * 2 + target
        columns = pl.ds(pl.multiple_of(block * BOTH, BOTH), BOTH)
        return pltpu.make_async_copy(inputs.at[:, columns], blocks.at[n], sems.at[n])

    first = pltpu.make_async_copy(grads, whole, sems.at[len(steps)])
    first.start()
    load(0).start()
    load(1).start()
    first.wait()
    for n in range(len(steps)):
        load(n).wait()
        if n + 2 < len(steps):
            load(n + 2).start()
        yield product(blocks[n], whole[...])


EARLY = (4, -3)
LATE = (-2, -1, 0)
KEPT = (3, 2, 1)


def early_kernel(swap, inputs, grads, _, keep4, away, blocks, whole, sems, both):
    core = place()[2]
    half = keep4.shape[1]
    turns = blocks_in_turn(EARLY, swap, inputs, grads, blocks, whole, sems)
    both[...] = next(turns)
    keep4[...] = both[:, pl.ds(pl.multiple_of(core * half, half), half)]
    other = both[:, pl.ds(pl.multiple_of((1 - core) * half, half), half)]
    encode(other[:ROWS], away.at[0, :, :half])
    encode(other[ROWS:], away.at[0, :, half:])
    total = next(turns)
    encode(total[:ROWS], away.at[1])
    encode(total[ROWS:], away.at[2])


def late_kernel(swap, inputs, grads, _, keep0, *refs):
    away, (blocks, whole, sems, both) = refs[:5], refs[5:]
    core = place()[2]
    turns = blocks_in_turn(LATE, swap, inputs, grads, blocks, whole, sems)
    for n in range(2):
        total = next(turns)
        encode(total[:ROWS], away[2 * n])
        encode(total[ROWS:], away[2 * n + 1])
    both[...] = next(turns)
    keep0[...] = both[pl.ds(pl.multiple_of(core * ROWS, ROWS), ROWS), :]
    encode(both[pl.ds(pl.multiple_of((1 - core) * ROWS, ROWS), ROWS), :], away[4])


def kept_kernel(swap, inputs, grads, _, keep3, keep2, keep1, blocks, whole, sems, sums, out_sems):
    keeps = (keep3, keep2, keep1)
    copies = []
    for n, total in enumerate(blocks_in_turn(KEPT, swap, inputs, grads, blocks, whole, sems)):
        sums[n] = total
        copies.append(pltpu.make_async_copy(sums.at[n], keeps[n], out_sems.at[n]))
        copies[n].start()
    for copy in copies:
        copy.wait()


def partial_sums(kernel, swap, inputs, grads, after, steps, outs, out_spec, scratch, name):
    tokens, breadth = grads.shape
    return pl.pallas_call(
        lambda *refs: kernel(swap, *refs),
        in_specs=[pl.BlockSpec(memory_space=pl.ANY)] * 3,
        out_specs=[out_spec] * len(outs),
        out_shape=[jax.ShapeDtypeStruct(*out) for out in outs],
        scratch_shapes=[
            pltpu.VMEM((steps, tokens, BOTH), BF),
            pltpu.VMEM((tokens, breadth), BF),
            pltpu.SemaphoreType.DMA((steps + 1,)),
            *scratch,
        ],
        compiler_params=pltpu.CompilerParams(vmem_limit_bytes=56 << 20),
        cost_estimate=pl.CostEstimate(
            flops=steps * 6 * BOTH * tokens * breadth,
            bytes_accessed=steps * (2 * BOTH * tokens + 2 * BOTH * breadth),
            transcendentals=0,
        ),
        name=name,
    )(inputs, grads, after)


def early_sums(swap, inputs, grads, after):
    breadth = grads.shape[1]
    outs = [((BOTH, breadth // 2), F32), ((3, ROWS + HEAD, breadth), I16)]
    return partial_sums(early_kernel, swap, inputs, grads, after, len(EARLY), outs,
                        pl.BlockSpec(memory_space=pltpu.VMEM), [pltpu.VMEM((BOTH, breadth), F32)], "early")


def late_sums(swap, inputs, grads, after):
    breadth = grads.shape[1]
    outs = [((ROWS, breadth), F32)] + [((ROWS + HEAD, breadth), I16)] * 5
    return partial_sums(late_kernel, swap, inputs, grads, after, len(LATE), outs,
                        pl.BlockSpec(memory_space=pltpu.VMEM), [pltpu.VMEM((BOTH, breadth), F32)], "late")


def kept_sums(swap, inputs, grads, after):
    breadth = grads.shape[1]
    return partial_sums(kept_kernel, swap, inputs, grads, after, len(KEPT), [((BOTH, breadth), F32)] * 3,
                        pl.BlockSpec(memory_space=pl.ANY),
                        [pltpu.VMEM((3, BOTH, breadth), F32), pltpu.SemaphoreType.DMA((3,))], "kept")


ANYWHERE = "any"


def call_local(kernel, args, specs, outs, name, scratch=()):
    def spec(arg, cut):
        if cut == ANYWHERE:
            return pl.BlockSpec(memory_space=pl.ANY)
        block, index = cut or (arg.shape, (0,) * arg.ndim)
        return pl.BlockSpec(block, lambda i: index)

    result = pl.pallas_call(
        kernel,
        grid=(1,),
        in_specs=[spec(arg, cut) for arg, cut in zip(args, specs)],
        out_specs=[pl.BlockSpec(shape, lambda i, n=len(shape): (0,) * n) for shape, _ in outs],
        out_shape=[jax.ShapeDtypeStruct(*out) for out in outs],
        scratch_shapes=list(scratch),
        compiler_params=pltpu.CompilerParams(vmem_limit_bytes=16 << 20),
        cost_estimate=pl.CostEstimate(flops=10 * BOTH * 512, bytes_accessed=10 * BOTH * 512, transcendentals=0),
        name=name,
    )(*args)
    return result


def decode_pair(low, high):
    return jnp.concatenate([decode(low), decode(high)], axis=0)


def first_hop_kernel(keep, other, out):
    half = keep.shape[1]
    encode(keep[...] + decode_pair(other.at[:, :half], other.at[:, half:]), out)


def second_hop_kernel(keep, low, high, arrived, _, out, total):
    half = arrived.shape[1]
    total[...] = keep[...] + decode_pair(low, high)
    mine = pl.ds(pl.multiple_of(place()[2] * half, half), half)
    total[:, mine] += decode(arrived)
    encode(total[...], out)


def later_hop_kernel(keep, low, high, arrived, *rest):
    out = rest[-1]
    encode(keep[...] + decode_pair(low, high) + decode(arrived), out)


def own_kernel(keep, other, out):
    encode(keep[...] + decode(other), out)


def meet_kernel(straight, aslant, keep, other, beside, kept, away, total):
    core = place()[2]
    total[...] = decode(straight) + decode(aslant)
    kept[...] = total[pl.ds(pl.multiple_of(core * ROWS, ROWS), ROWS), :] + keep[...] + decode(other) + decode(beside)
    encode(total[pl.ds(pl.multiple_of((1 - core) * ROWS, ROWS), ROWS), :], away)


def replica_sum(inputs, grads):
    breadth = grads.shape[1]
    tall, short = BOTH + HEAD, ROWS + HEAD

    def send(array, pairs):
        return lax.ppermute(array, "fsdp", pairs)

    def unit(n):
        return (None, short, breadth), (n, 0, 0)

    def first_hop(keep, other):
        return call_local(first_hop_kernel, (keep, other), (None, unit(0)), [((tall, breadth // 2), I16)], "hop1")[0]

    def later_hop(step, keep, early, late, arrived, after):
        if step == 2:
            others, cuts = (early, early), (unit(1), unit(2))
        else:
            others, cuts = late[2 * step - 6:2 * step - 4], (None, None)
        scratch = [pltpu.VMEM((BOTH, breadth), F32)] if step == 2 else []
        return call_local(
            second_hop_kernel if step == 2 else later_hop_kernel,
            (keep, *others, arrived, after), (None, *cuts, None, ANYWHERE),
            [((tall, breadth), I16)], "hop%d" % step, scratch)[0]

    keep4_a, away = early_sums(True, inputs, grads, inputs)
    early_a = send(away, WITHIN)
    keep4_b, away = early_sums(False, inputs, grads, away)
    early_b = send(away, WITHIN)
    ring_a = first_hop(keep4_a, early_a)
    ring_b = first_hop(keep4_b, early_b)
    kept_a = kept_sums(True, inputs, grads, ring_a)
    kept_b = kept_sums(False, inputs, grads, kept_a[0])
    ring_a = later_hop(2, kept_a[0], early_a, None, send(ring_a, ALONG), kept_a[0])
    ring_b = later_hop(2, kept_b[0], early_b, None, send(ring_b, ALONG), kept_b[0])
    keep0_a, *away = late_sums(True, inputs, grads, ring_a)
    late_a = [send(part, WITHIN) for part in away]
    keep0_b, *away = late_sums(False, inputs, grads, ring_b)
    late_b = [send(part, WITHIN) for part in away]
    own_a = call_local(own_kernel, (keep0_a, late_a[4]), (None, None), [((short, breadth), I16)], "own")[0]
    beside = send(own_a, BESIDE)
    ring_a = later_hop(3, kept_a[1], None, late_a, send(ring_a, ALONG), own_a)
    ring_b = later_hop(3, kept_b[1], None, late_b, send(ring_b, ALONG), own_a)
    ring_a = later_hop(4, kept_a[2], None, late_a, send(ring_a, ALONG), own_a)
    ring_b = later_hop(4, kept_b[2], None, late_b, send(ring_b, ALONG), beside)
    ring_a, ring_b = send(ring_a, ASLANT), send(ring_b, ALONG)
    kept, away = call_local(
        meet_kernel, (ring_b, ring_a, keep0_b, late_b[4], beside), (None,) * 5,
        [((ROWS, breadth), F32), ((short, breadth), I16)], "meet", [pltpu.VMEM((BOTH, breadth), F32)])
    return kept, send(away, WITHIN)


def spread(row, height):
    return jnp.concatenate([jnp.broadcast_to(row, (HEAD, row.shape[1])).astype(BF)] * (height // HEAD), axis=0)


def row_numbers(height, width):
    return lax.broadcasted_iota(jnp.int32, (height, width), 0).astype(F32).astype(BF)


def pick_kernel(kept, other, momentum, places, rows, rows_t, cols, cols_t, new_moment, payload, coef, sparse):
    grad = kept[...] + decode(other)
    moment = 0.9 * momentum[...] + grad
    coef[...] = right_product(left_product(rows, moment), cols_t)
    tile_rows, tile_cols = momentum.shape[0] // CH, momentum.shape[1] // CH
    group = 4
    tiles = tile_rows * tile_cols
    width = group * SLOTS
    numbers = row_numbers(group * CH, width)
    one, none = jnp.ones((), BF), jnp.zeros((), BF)
    for i in range(tile_rows):
        for h in range(tile_cols // group):
            first = i * tile_cols + h * group
            part = [places[first + n:first + n + 1, :] for n in range(group)]
            row_code = (jnp.concatenate(part, axis=1) >> 6).astype(F32)
            col_code = jnp.concatenate([(p & 63) + CH * n for n, p in enumerate(part)], axis=1).astype(F32)
            col_hot = jnp.where(numbers == spread(col_code, group * CH), one, none)
            row_hot = jnp.where(numbers[:CH] == spread(row_code, CH), one, none)
            block = coef[i * CH:(i + 1) * CH, h * group * CH:(h + 1) * group * CH]
            high, low = split(block)
            chosen = dot(high, col_hot) + dot(low, col_hot)
            value = jnp.sum(chosen * row_hot.astype(F32), axis=0, keepdims=True)
            for n in range(group):
                for r in range(payload.shape[0]):
                    payload[r, first + n:first + n + 1, :] = value[:, n * SLOTS:(n + 1) * SLOTS]
            sparse[i * CH:(i + 1) * CH, h * group * CH:(h + 1) * group * CH] = block * dot_nt(row_hot, col_hot)
    for r in range(payload.shape[0]):
        payload[r, tiles:, :] = places[...].astype(F32)
    new_moment[...] = moment - right_product(left_product(rows_t, sparse[...]), cols)


def decode_kernel(gathered, rows_t, cols, step_dir, total):
    reps = gathered.shape[0]
    tiles = gathered.shape[1] // 2
    tile_cols = total.shape[1] // CH
    numbers = row_numbers(CH, SLOTS)
    one, none = jnp.ones((), BF), jnp.zeros((), BF)
    parts = []
    for r in range(reps):
        high, low = split(gathered[r, :tiles, :])
        place = gathered[r, tiles:, :].astype(jnp.int32)
        parts.append([high.astype(F32), low.astype(F32), (place >> 6).astype(F32), (place & 63).astype(F32)])
    for pair in range(tiles // 2):
        blocks = []
        for t in (2 * pair, 2 * pair + 1):
            highs, lows, hots = [], [], []
            for r in range(reps):
                high, low, row_code, col_code = (spread(part[t:t + 1, :], CH) for part in parts[r])
                in_row = numbers == row_code
                highs.append(jnp.where(in_row, high, none))
                lows.append(jnp.where(in_row, low, none))
                hots.append(jnp.where(numbers == col_code, one, none))
            both = jnp.concatenate([jnp.concatenate(highs, axis=1), jnp.concatenate(lows, axis=1)], axis=0)
            out = dot_nt(both, jnp.concatenate(hots, axis=1))
            blocks.append(out[:CH] + out[CH:])
        i, j = (2 * pair) // tile_cols, (2 * pair) % tile_cols
        total[i * CH:(i + 1) * CH, j * CH:(j + 2) * CH] = jnp.concatenate(blocks, axis=1)
    decoded = right_product(left_product(rows_t, total[...]), cols)
    step_dir[...] = decoded * lax.rsqrt(decoded * decoded + 0.04)


def body(activations, out_grads, momentum, indices, counts):
    reps = lax.axis_size("rep")
    table = cosine_table(CH)
    rows = np.kron(np.eye(3), table)
    cols = np.kron(np.eye(4), table)
    rows, rows_t, cols, cols_t = (jnp.asarray(two_terms(m)) for m in (rows, rows.T, cols, cols.T))
    height, breadth = momentum.shape[1:]
    tiles = (height // CH) * (breadth // CH)
    live = lax.broadcasted_iota(jnp.int32, indices.shape[1:], 2) < counts[0]
    places = jnp.where(live, indices[0], -1).reshape(tiles, SLOTS)
    kept, other = replica_sum(activations[0], out_grads[0])
    new_moment, payload = pl.pallas_call(
        pick_kernel,
        out_shape=[
            jax.ShapeDtypeStruct((height, breadth), F32),
            jax.ShapeDtypeStruct((reps, 2 * tiles, SLOTS), F32),
        ],
        scratch_shapes=[pltpu.VMEM((height, breadth), F32), pltpu.VMEM((height, breadth), F32)],
        compiler_params=pltpu.CompilerParams(vmem_limit_bytes=32 << 20),
        name="pick",
    )(kept, other, momentum[0], places, rows, rows_t, cols, cols_t)
    gathered = lax.all_to_all(payload, "rep", 0, 0)
    step_dir = pl.pallas_call(
        decode_kernel,
        out_shape=jax.ShapeDtypeStruct((height, breadth), F32),
        scratch_shapes=[pltpu.VMEM((height, breadth), F32)],
        compiler_params=pltpu.CompilerParams(vmem_limit_bytes=32 << 20),
        name="decode",
    )(gathered, rows_t, cols)
    return (new_moment[None], step_dir)


def solution(mesh):
    placed = (
        P("rep", "fsdp", None),
        P("rep", "fsdp", None),
        P("rep", "fsdp", None),
        P("rep", "fsdp", None, None),
        P("rep"),
    )
    return jax.shard_map(
        body,
        mesh=mesh,
        in_specs=placed,
        out_specs=(P("rep", "fsdp", None), P("fsdp", None)),
        check_vma=False,
    )
```

```python
import math

import jax
import jax.numpy as jnp
import numpy as np
from jax import lax
from jax.experimental import pallas as pl
from jax.experimental.pallas import tpu as pltpu
from jax.sharding import PartitionSpec as P

CH = 64
SLOTS = 128
BF = jnp.bfloat16
F32 = jnp.float32
I16 = jnp.int16
HEAD = 16
RINGS = 8
ROWS = 192
BOTH = 2 * ROWS


def cosine_table(side):
    freq = np.arange(side, dtype=np.float64)[:, None]
    place = np.arange(side, dtype=np.float64)[None, :]
    table = np.cos(math.pi * (2.0 * place + 1.0) * freq / (2.0 * side)) * math.sqrt(2.0 / side)
    return np.where(freq < 0.5, table * math.sqrt(0.5), table)


def two_terms(matrix):
    high = matrix.astype(np.float32).astype(BF)
    low = (matrix - high.astype(np.float64)).astype(np.float32).astype(BF)
    return np.stack([high, low])


def split(x):
    high = x.astype(BF)
    return high, (x - high.astype(F32)).astype(BF)


def dot(a, b):
    return jnp.dot(a, b, preferred_element_type=F32)


def dot_nt(a, b):
    return lax.dot_general(a, b, (((1,), (1,)), ((), ())), preferred_element_type=F32)


def left_product(table, x):
    high, low = split(x)
    height = table.shape[1]
    both = dot(jnp.concatenate([table[0], table[1]], axis=0), high)
    return both[:height] + (both[height:] + dot(table[0], low))


def right_product(x, table):
    width = table.shape[-1]
    height = x.shape[0]
    pieces = []
    for start in range(0, x.shape[1], width):
        high, low = split(x[:, start:start + width])
        both = dot(jnp.concatenate([high, low], axis=0), table[0])
        pieces.append(both[:height] + (both[height:] + dot(high, table[1])))
    return jnp.concatenate(pieces, axis=1)


def encode(x, out):
    top = jnp.max(jnp.abs(x), axis=0, keepdims=True)
    code = jnp.ceil(128.0 * jnp.log2(jnp.maximum(top, 1e-30))) + 1.0
    scale = 32767.0 * jnp.exp2(code * (-1.0 / 128.0))
    height = x.shape[0]
    out[:height, :] = jnp.round(x * scale).astype(jnp.int32).astype(I16)
    out[height:, :] = jnp.broadcast_to(code, (HEAD, x.shape[1])).astype(jnp.int32).astype(I16)


def decode(ref):
    height = ref.shape[0] - HEAD
    code = ref[height:, :].astype(jnp.int32).astype(F32)[:1, :]
    scale = jnp.exp2(code * (1.0 / 128.0)) * (1.0 / 32767.0)
    return ref[:height, :].astype(jnp.int32).astype(F32) * scale


def place():
    me = lax.axis_index("fsdp")
    return me // 4, lax.rem(me // 2, 2), lax.rem(me, 2)


def route(move):
    pairs = []
    for source in range(4 * RINGS):
        z, y, core = move(source // 4, (source // 2) % 2, source % 2)
        pairs.append((source, ((z % RINGS) * 2 + y) * 2 + core))
    return pairs


ALONG = route(lambda z, y, c: (z + 1 - 2 * c, y, c))
ASLANT = route(lambda z, y, c: (z + 1 - 2 * c, 1 - y, c))
BESIDE = route(lambda z, y, c: (z, 1 - y, c))
WITHIN = route(lambda z, y, c: (z, y, 1 - c))


def product(left, right):
    return lax.dot_general(left, right, (((0,), (0,)), ((), ())), preferred_element_type=F32)


EARLY = (4, -3)
LATE = (-2, -1, 0)
KEPT = (3, 2, 1)


def loads(steps, swap, inputs, blocks, sems):
    z, y, core = place()
    target = 1 - y if swap else y
    copies = []
    for n, step in enumerate(steps):
        block = lax.rem(z + step * (1 - 2 * core) + RINGS, RINGS) * 2 + target
        columns = pl.ds(pl.multiple_of(block * BOTH, BOTH), BOTH)
        copies.append(pltpu.make_async_copy(inputs.at[:, columns], blocks.at[n], sems.at[n]))
    return copies


def early_part(core, blocks, grads, keep4, away, both, ready=None):
    half = keep4.shape[1]
    both[...] = product(blocks[0], grads[...])
    keep4[...] = both[:, pl.ds(pl.multiple_of(core * half, half), half)]
    other = both[:, pl.ds(pl.multiple_of((1 - core) * half, half), half)]
    encode(other[:ROWS], away.at[0, :, :half])
    encode(other[ROWS:], away.at[0, :, half:])
    if ready is not None:
        ready.wait()
    total = product(blocks[1], grads[...])
    encode(total[:ROWS], away.at[1])
    encode(total[ROWS:], away.at[2])


def first_kernel(inputs, grads, keep4, away, kept_grads, ahead, blocks, both, sems, ahead_sems, grad_sem):
    whole = pltpu.make_async_copy(grads, kept_grads, grad_sem)
    mine = loads(EARLY, True, inputs, blocks, sems)
    more = loads(EARLY, False, inputs, ahead, ahead_sems)
    whole.start()
    mine[0].start()
    mine[1].start()
    whole.wait()
    mine[0].wait()
    for copy in more:
        copy.start()
    early_part(place()[2], blocks, kept_grads, keep4, away, both, mine[1])
    for copy in more:
        copy.wait()


def early_kernel(inputs, grads, blocks, _, keep4, away, ahead, both, sems):
    more = loads(KEPT, True, inputs, ahead, sems)
    for copy in more:
        copy.start()
    early_part(place()[2], blocks, grads, keep4, away, both)
    for copy in more:
        copy.wait()


def kept_kernel(then, inputs, grads, blocks, _, *refs):
    keeps, (ahead, sums, out_sems, sems) = refs[:3], refs[3:]
    more = loads(*then, inputs, ahead, sems)
    for copy in more:
        copy.start()
    copies = []
    for n, keep in enumerate(keeps):
        sums[n] = product(blocks[n], grads[...])
        copies.append(pltpu.make_async_copy(sums.at[n], keep, out_sems.at[n]))
        copies[n].start()
    for copy in copies + more:
        copy.wait()


def late_kernel(then, inputs, grads, blocks, _, keep0, *refs):
    away, refs = refs[:5], refs[5:]
    more = loads(*then, inputs, refs[0], refs[2]) if then else []
    both = refs[1] if then else refs[0]
    for copy in more:
        copy.start()
    core = place()[2]
    for n in range(2):
        total = product(blocks[n], grads[...])
        encode(total[:ROWS], away[2 * n])
        encode(total[ROWS:], away[2 * n + 1])
    both[...] = product(blocks[2], grads[...])
    keep0[...] = both[pl.ds(pl.multiple_of(core * ROWS, ROWS), ROWS), :]
    encode(both[pl.ds(pl.multiple_of((1 - core) * ROWS, ROWS), ROWS), :], away[4])
    for copy in more:
        copy.wait()


def partial_sums(kernel, args, outs, scratch, steps, name):
    tokens, breadth = args[1][0].shape
    return pl.pallas_call(
        kernel,
        in_specs=[pl.BlockSpec(memory_space=space) for _, space in args],
        out_specs=[pl.BlockSpec(memory_space=space) for _, _, space in outs],
        out_shape=[jax.ShapeDtypeStruct(shape, kind) for shape, kind, _ in outs],
        scratch_shapes=scratch,
        compiler_params=pltpu.CompilerParams(vmem_limit_bytes=46 << 20),
        cost_estimate=pl.CostEstimate(
            flops=steps * 6 * BOTH * tokens * breadth,
            bytes_accessed=steps * (2 * BOTH * tokens + 2 * BOTH * breadth),
            transcendentals=0,
        ),
        name=name,
    )(*(array for array, _ in args))


def all_sums(inputs, grads):
    tokens, breadth = grads.shape
    vmem = pltpu.VMEM
    tall, short = (BOTH, breadth), (ROWS + HEAD, breadth)

    def fetched(steps):
        return ((len(steps), tokens, BOTH), BF, vmem)

    def sems(steps):
        return pltpu.SemaphoreType.DMA((len(steps),))

    early = [((BOTH, breadth // 2), F32, vmem), ((3, *short), I16, vmem)]
    kept = [(tall, F32, pl.ANY)] * 3
    late = [((ROWS, breadth), F32, vmem)] + [(short, I16, vmem)] * 5
    both = vmem(tall, F32)

    def args(blocks, behind):
        return (inputs, pl.ANY), (held, vmem), (blocks, vmem), (behind, pl.ANY)

    keep4, away, held, ahead = partial_sums(
        first_kernel, ((inputs, pl.ANY), (grads, pl.ANY)), early + [(grads.shape, BF, vmem), fetched(EARLY)],
        [vmem((len(EARLY), tokens, BOTH), BF), both, sems(EARLY), sems(EARLY), pltpu.SemaphoreType.DMA], 3, "early")
    behind = yield keep4, away
    keep4, away, ahead = partial_sums(
        early_kernel, args(ahead, behind), early + [fetched(KEPT)], [both, sems(KEPT)], 2, "early")
    behind = yield keep4, away
    sums = [vmem((3, *tall), F32), sems(KEPT)]
    *keeps, ahead = partial_sums(
        lambda *refs: kept_kernel((KEPT, False), *refs), args(ahead, behind), kept + [fetched(KEPT)], sums + [sems(KEPT)], 3, "kept")
    behind = yield keeps
    *keeps, ahead = partial_sums(
        lambda *refs: kept_kernel((LATE, True), *refs), args(ahead, behind), kept + [fetched(LATE)], sums + [sems(LATE)], 3, "kept")
    behind = yield keeps
    keep0, *away, ahead = partial_sums(
        lambda *refs: late_kernel((LATE, False), *refs), args(ahead, behind), late + [fetched(LATE)], [both, sems(LATE)], 3, "late")
    behind = yield keep0, away
    keep0, *away = partial_sums(
        lambda *refs: late_kernel(None, *refs), args(ahead, behind), late, [both], 3, "late")
    yield keep0, away


ANYWHERE = "any"


def call_local(kernel, args, specs, outs, name, scratch=()):
    def spec(arg, cut):
        if cut == ANYWHERE:
            return pl.BlockSpec(memory_space=pl.ANY)
        block, index = cut or (arg.shape, (0,) * arg.ndim)
        return pl.BlockSpec(block, lambda i: index)

    result = pl.pallas_call(
        kernel,
        grid=(1,),
        in_specs=[spec(arg, cut) for arg, cut in zip(args, specs)],
        out_specs=[pl.BlockSpec(shape, lambda i, n=len(shape): (0,) * n) for shape, _ in outs],
        out_shape=[jax.ShapeDtypeStruct(*out) for out in outs],
        scratch_shapes=list(scratch),
        compiler_params=pltpu.CompilerParams(vmem_limit_bytes=16 << 20),
        cost_estimate=pl.CostEstimate(flops=10 * BOTH * 512, bytes_accessed=10 * BOTH * 512, transcendentals=0),
        name=name,
    )(*args)
    return result


def decode_pair(low, high):
    return jnp.concatenate([decode(low), decode(high)], axis=0)


def first_hop_kernel(keep, other, out):
    half = keep.shape[1]
    encode(keep[...] + decode_pair(other.at[:, :half], other.at[:, half:]), out)


def second_hop_kernel(keep, low, high, arrived, _, out, total):
    half = arrived.shape[1]
    total[...] = keep[...] + decode_pair(low, high)
    mine = pl.ds(pl.multiple_of(place()[2] * half, half), half)
    total[:, mine] += decode(arrived)
    encode(total[...], out)


def later_hop_kernel(keep, low, high, arrived, *rest):
    out = rest[-1]
    encode(keep[...] + decode_pair(low, high) + decode(arrived), out)


def own_kernel(keep, other, out):
    encode(keep[...] + decode(other), out)


def meet_kernel(straight, aslant, keep, other, beside, kept, away, total):
    core = place()[2]
    total[...] = decode(straight) + decode(aslant)
    kept[...] = total[pl.ds(pl.multiple_of(core * ROWS, ROWS), ROWS), :] + keep[...] + decode(other) + decode(beside)
    encode(total[pl.ds(pl.multiple_of((1 - core) * ROWS, ROWS), ROWS), :], away)


def replica_sum(inputs, grads):
    breadth = grads.shape[1]
    tall, short = BOTH + HEAD, ROWS + HEAD

    def send(array, pairs):
        return lax.ppermute(array, "fsdp", pairs)

    def unit(n):
        return (None, short, breadth), (n, 0, 0)

    def first_hop(keep, other):
        return call_local(first_hop_kernel, (keep, other), (None, unit(0)), [((tall, breadth // 2), I16)], "hop1")[0]

    def later_hop(step, keep, early, late, arrived, after):
        if step == 2:
            others, cuts = (early, early), (unit(1), unit(2))
        else:
            others, cuts = late[2 * step - 6:2 * step - 4], (None, None)
        scratch = [pltpu.VMEM((BOTH, breadth), F32)] if step == 2 else []
        return call_local(
            second_hop_kernel if step == 2 else later_hop_kernel,
            (keep, *others, arrived, after), (None, *cuts, None, ANYWHERE),
            [((tall, breadth), I16)], "hop%d" % step, scratch)[0]

    sums = all_sums(inputs, grads)
    keep4_a, away = next(sums)
    early_a = send(away, WITHIN)
    keep4_b, away = sums.send(away)
    early_b = send(away, WITHIN)
    ring_a = first_hop(keep4_a, early_a)
    ring_b = first_hop(keep4_b, early_b)
    kept_a = sums.send(ring_a)
    kept_b = sums.send(kept_a[0])
    ring_a = later_hop(2, kept_a[0], early_a, None, send(ring_a, ALONG), kept_a[0])
    ring_b = later_hop(2, kept_b[0], early_b, None, send(ring_b, ALONG), kept_b[0])
    keep0_a, away = sums.send(ring_a)
    late_a = [send(part, WITHIN) for part in away]
    keep0_b, away = sums.send(ring_b)
    late_b = [send(part, WITHIN) for part in away]
    own_a = call_local(own_kernel, (keep0_a, late_a[4]), (None, None), [((short, breadth), I16)], "own")[0]
    beside = send(own_a, BESIDE)
    ring_a = later_hop(3, kept_a[1], None, late_a, send(ring_a, ALONG), own_a)
    ring_b = later_hop(3, kept_b[1], None, late_b, send(ring_b, ALONG), own_a)
    ring_a = later_hop(4, kept_a[2], None, late_a, send(ring_a, ALONG), own_a)
    ring_b = later_hop(4, kept_b[2], None, late_b, send(ring_b, ALONG), beside)
    ring_a, ring_b = send(ring_a, ASLANT), send(ring_b, ALONG)
    kept, away = call_local(
        meet_kernel, (ring_b, ring_a, keep0_b, late_b[4], beside), (None,) * 5,
        [((ROWS, breadth), F32), ((short, breadth), I16)], "meet", [pltpu.VMEM((BOTH, breadth), F32)])
    return kept, send(away, WITHIN)


def spread(row, height):
    return jnp.concatenate([jnp.broadcast_to(row, (HEAD, row.shape[1])).astype(BF)] * (height // HEAD), axis=0)


def row_numbers(height, width):
    return lax.broadcasted_iota(jnp.int32, (height, width), 0).astype(F32).astype(BF)


def pick_kernel(kept, other, momentum, places, rows, rows_t, cols, cols_t, new_moment, payload, coef, sparse):
    grad = kept[...] + decode(other)
    moment = 0.9 * momentum[...] + grad
    coef[...] = right_product(left_product(rows, moment), cols_t)
    tile_rows, tile_cols = momentum.shape[0] // CH, momentum.shape[1] // CH
    group = 4
    tiles = tile_rows * tile_cols
    width = group * SLOTS
    numbers = row_numbers(group * CH, width)
    one, none = jnp.ones((), BF), jnp.zeros((), BF)
    for i in range(tile_rows):
        for h in range(tile_cols // group):
            first = i * tile_cols + h * group
            part = [places[first + n:first + n + 1, :] for n in range(group)]
            row_code = (jnp.concatenate(part, axis=1) >> 6).astype(F32)
            col_code = jnp.concatenate([(p & 63) + CH * n for n, p in enumerate(part)], axis=1).astype(F32)
            col_hot = jnp.where(numbers == spread(col_code, group * CH), one, none)
            row_hot = jnp.where(numbers[:CH] == spread(row_code, CH), one, none)
            block = coef[i * CH:(i + 1) * CH, h * group * CH:(h + 1) * group * CH]
            high, low = split(block)
            chosen = dot(jnp.concatenate([high, low], axis=0), col_hot)
            chosen = chosen[:CH] + chosen[CH:]
            value = jnp.sum(chosen * row_hot.astype(F32), axis=0, keepdims=True)
            for n in range(group):
                for r in range(payload.shape[0]):
                    payload[r, first + n:first + n + 1, :] = value[:, n * SLOTS:(n + 1) * SLOTS]
            sparse[i * CH:(i + 1) * CH, h * group * CH:(h + 1) * group * CH] = block * dot_nt(row_hot, col_hot)
    for r in range(payload.shape[0]):
        payload[r, tiles:, :] = places[...].astype(F32)
    new_moment[...] = moment - right_product(left_product(rows_t, sparse[...]), cols)


def decode_kernel(gathered, rows_t, cols, step_dir, total):
    reps = gathered.shape[0]
    tiles = gathered.shape[1] // 2
    tile_cols = total.shape[1] // CH
    numbers = row_numbers(CH, SLOTS)
    one, none = jnp.ones((), BF), jnp.zeros((), BF)
    parts = []
    for r in range(reps):
        high, low = split(gathered[r, :tiles, :])
        place = gathered[r, tiles:, :].astype(jnp.int32)
        parts.append([high.astype(F32), low.astype(F32), (place >> 6).astype(F32), (place & 63).astype(F32)])
    for pair in range(tiles // 2):
        blocks = []
        for t in (2 * pair, 2 * pair + 1):
            highs, lows, hots = [], [], []
            for r in range(reps):
                high, low, row_code, col_code = (spread(part[t:t + 1, :], CH) for part in parts[r])
                in_col = numbers == col_code
                highs.append(jnp.where(in_col, high, none))
                lows.append(jnp.where(in_col, low, none))
                hots.append(jnp.where(numbers == row_code, one, none))
            both = jnp.concatenate([jnp.concatenate(highs, axis=1), jnp.concatenate(lows, axis=1)], axis=0)
            out = dot_nt(jnp.concatenate(hots, axis=1), both)
            blocks.append(out[:, :CH] + out[:, CH:])
        i, j = (2 * pair) // tile_cols, (2 * pair) % tile_cols
        total[i * CH:(i + 1) * CH, j * CH:(j + 2) * CH] = jnp.concatenate(blocks, axis=1)
    decoded = right_product(left_product(rows_t, total[...]), cols)
    step_dir[...] = decoded * lax.rsqrt(decoded * decoded + 0.04)


def body(activations, out_grads, momentum, indices, counts):
    reps = lax.axis_size("rep")
    table = cosine_table(CH)
    rows = np.kron(np.eye(3), table)
    cols = np.kron(np.eye(4), table)
    rows, rows_t, cols, cols_t = (jnp.asarray(two_terms(m)) for m in (rows, rows.T, cols, cols.T))
    height, breadth = momentum.shape[1:]
    tiles = (height // CH) * (breadth // CH)
    live = lax.broadcasted_iota(jnp.int32, indices.shape[1:], 2) < counts[0]
    places = jnp.where(live, indices[0], -1).reshape(tiles, SLOTS)
    kept, other = replica_sum(activations[0], out_grads[0])
    new_moment, payload = pl.pallas_call(
        pick_kernel,
        out_shape=[
            jax.ShapeDtypeStruct((height, breadth), F32),
            jax.ShapeDtypeStruct((reps, 2 * tiles, SLOTS), F32),
        ],
        scratch_shapes=[pltpu.VMEM((height, breadth), F32), pltpu.VMEM((height, breadth), F32)],
        compiler_params=pltpu.CompilerParams(vmem_limit_bytes=32 << 20),
        name="pick",
    )(kept, other, momentum[0], places, rows, rows_t, cols, cols_t)
    gathered = lax.all_to_all(payload, "rep", 0, 0)
    step_dir = pl.pallas_call(
        decode_kernel,
        out_shape=jax.ShapeDtypeStruct((height, breadth), F32),
        scratch_shapes=[pltpu.VMEM((height, breadth), F32)],
        compiler_params=pltpu.CompilerParams(vmem_limit_bytes=32 << 20),
        name="decode",
    )(gathered, rows_t, cols)
    return (new_moment[None], step_dir)


def solution(mesh):
    placed = (
        P("rep", "fsdp", None),
        P("rep", "fsdp", None),
        P("rep", "fsdp", None),
        P("rep", "fsdp", None, None),
        P("rep"),
    )
    return jax.shard_map(
        body,
        mesh=mesh,
        in_specs=placed,
        out_specs=(P("rep", "fsdp", None), P("fsdp", None)),
        check_vma=False,
    )
```

```python
import math

import jax
import jax.numpy as jnp
import numpy as np
from jax import lax
from jax.experimental import pallas as pl
from jax.experimental.pallas import tpu as pltpu
from jax.sharding import PartitionSpec as P

CH = 64
SLOTS = 128
BF = jnp.bfloat16
F32 = jnp.float32
I16 = jnp.int16
HEAD = 16
RINGS = 8
ROWS = 192
BOTH = 2 * ROWS


def cosine_table(side):
    freq = np.arange(side, dtype=np.float64)[:, None]
    place = np.arange(side, dtype=np.float64)[None, :]
    table = np.cos(math.pi * (2.0 * place + 1.0) * freq / (2.0 * side)) * math.sqrt(2.0 / side)
    return np.where(freq < 0.5, table * math.sqrt(0.5), table)


def two_terms(matrix):
    high = matrix.astype(np.float32).astype(BF)
    low = (matrix - high.astype(np.float64)).astype(np.float32).astype(BF)
    return np.stack([high, low])


def split(x):
    high = x.astype(BF)
    return high, (x - high.astype(F32)).astype(BF)


def dot(a, b):
    return jnp.dot(a, b, preferred_element_type=F32)


def dot_nt(a, b):
    return lax.dot_general(a, b, (((1,), (1,)), ((), ())), preferred_element_type=F32)


def left_product(table, x):
    high, low = split(x)
    height = table.shape[1]
    both = dot(jnp.concatenate([table[0], table[1]], axis=0), high)
    return both[:height] + (both[height:] + dot(table[0], low))


def right_product(x, table):
    width = table.shape[-1]
    height = x.shape[0]
    pieces = []
    for start in range(0, x.shape[1], width):
        high, low = split(x[:, start:start + width])
        both = dot(jnp.concatenate([high, low], axis=0), table[0])
        pieces.append(both[:height] + (both[height:] + dot(high, table[1])))
    return jnp.concatenate(pieces, axis=1)


def encode(x, out):
    top = jnp.max(jnp.abs(x), axis=0, keepdims=True)
    code = jnp.ceil(128.0 * jnp.log2(jnp.maximum(top, 1e-30))) + 1.0
    scale = 32767.0 * jnp.exp2(code * (-1.0 / 128.0))
    height = x.shape[0]
    out[:height, :] = jnp.round(x * scale).astype(jnp.int32).astype(I16)
    out[height:, :] = jnp.broadcast_to(code, (HEAD, x.shape[1])).astype(jnp.int32).astype(I16)


def decode(ref):
    height = ref.shape[0] - HEAD
    code = ref[height:, :].astype(jnp.int32).astype(F32)[:1, :]
    scale = jnp.exp2(code * (1.0 / 128.0)) * (1.0 / 32767.0)
    return ref[:height, :].astype(jnp.int32).astype(F32) * scale


def place():
    me = lax.axis_index("fsdp")
    return me // 4, lax.rem(me // 2, 2), lax.rem(me, 2)


def route(move):
    pairs = []
    for source in range(4 * RINGS):
        z, y, core = move(source // 4, (source // 2) % 2, source % 2)
        pairs.append((source, ((z % RINGS) * 2 + y) * 2 + core))
    return pairs


ALONG = route(lambda z, y, c: (z + 1 - 2 * c, y, c))
ACROSS = route(lambda z, y, c: (z + 1 - 2 * c, y, 1 - c))
ASLANT = route(lambda z, y, c: (z + 1 - 2 * c, 1 - y, c))
ASLANT_ACROSS = route(lambda z, y, c: (z + 1 - 2 * c, 1 - y, 1 - c))
BESIDE = route(lambda z, y, c: (z, 1 - y, c))
WITHIN = route(lambda z, y, c: (z, y, 1 - c))


def product(left, right):
    return lax.dot_general(left, right, (((0,), (0,)), ((), ())), preferred_element_type=F32)


EARLY = (4, -3)
LATE = (-2, -1, 0)
KEPT = (3, 2, 1)


def loads(steps, swap, inputs, blocks, sems):
    z, y, core = place()
    target = 1 - y if swap else y
    copies = []
    for n, step in enumerate(steps):
        block = lax.rem(z + step * (1 - 2 * core) + RINGS, RINGS) * 2 + target
        columns = pl.ds(pl.multiple_of(block * BOTH, BOTH), BOTH)
        copies.append(pltpu.make_async_copy(inputs.at[:, columns], blocks.at[n], sems.at[n]))
    return copies


def early_part(core, blocks, grads, keep4, away, both, ready=None):
    half = keep4.shape[1]
    both[...] = product(blocks[0], grads[...])
    keep4[...] = both[:, pl.ds(pl.multiple_of(core * half, half), half)]
    other = both[:, pl.ds(pl.multiple_of((1 - core) * half, half), half)]
    encode(other[:ROWS], away.at[0, :, :half])
    encode(other[ROWS:], away.at[0, :, half:])
    if ready is not None:
        ready.wait()
    total = product(blocks[1], grads[...])
    encode(total[:ROWS], away.at[1])
    encode(total[ROWS:], away.at[2])


def first_kernel(inputs, grads, keep4, away, kept_grads, ahead, blocks, both, sems, ahead_sems, grad_sem):
    whole = pltpu.make_async_copy(grads, kept_grads, grad_sem)
    mine = loads(EARLY, True, inputs, blocks, sems)
    more = loads(EARLY, False, inputs, ahead, ahead_sems)
    whole.start()
    mine[0].start()
    mine[1].start()
    whole.wait()
    mine[0].wait()
    for copy in more:
        copy.start()
    early_part(place()[2], blocks, kept_grads, keep4, away, both, mine[1])
    for copy in more:
        copy.wait()


def early_kernel(inputs, grads, blocks, _, keep4, away, ahead, both, sems):
    more = loads(KEPT, True, inputs, ahead, sems)
    for copy in more:
        copy.start()
    early_part(place()[2], blocks, grads, keep4, away, both)
    for copy in more:
        copy.wait()


def kept_kernel(then, inputs, grads, blocks, _, *refs):
    keeps, (ahead, sums, out_sems, sems) = refs[:3], refs[3:]
    more = loads(*then, inputs, ahead, sems)
    for copy in more:
        copy.start()
    copies = []
    for n, keep in enumerate(keeps):
        sums[n] = product(blocks[n], grads[...])
        copies.append(pltpu.make_async_copy(sums.at[n], keep, out_sems.at[n]))
        copies[n].start()
    for copy in copies + more:
        copy.wait()


def late_kernel(then, inputs, grads, blocks, _, keep0, *refs):
    away, refs = refs[:5], refs[5:]
    more = loads(*then, inputs, refs[0], refs[2]) if then else []
    both = refs[1] if then else refs[0]
    for copy in more:
        copy.start()
    core = place()[2]
    for n in range(2):
        total = product(blocks[n], grads[...])
        encode(total[:ROWS], away[2 * n])
        encode(total[ROWS:], away[2 * n + 1])
    both[...] = product(blocks[2], grads[...])
    keep0[...] = both[pl.ds(pl.multiple_of(core * ROWS, ROWS), ROWS), :]
    encode(both[pl.ds(pl.multiple_of((1 - core) * ROWS, ROWS), ROWS), :], away[4])
    for copy in more:
        copy.wait()


def partial_sums(kernel, args, outs, scratch, steps, name):
    tokens, breadth = args[1][0].shape
    return pl.pallas_call(
        kernel,
        in_specs=[pl.BlockSpec(memory_space=space) for _, space in args],
        out_specs=[pl.BlockSpec(memory_space=space) for _, _, space in outs],
        out_shape=[jax.ShapeDtypeStruct(shape, kind) for shape, kind, _ in outs],
        scratch_shapes=scratch,
        compiler_params=pltpu.CompilerParams(vmem_limit_bytes=46 << 20),
        cost_estimate=pl.CostEstimate(
            flops=steps * 6 * BOTH * tokens * breadth,
            bytes_accessed=steps * (2 * BOTH * tokens + 2 * BOTH * breadth),
            transcendentals=0,
        ),
        name=name,
    )(*(array for array, _ in args))


def all_sums(inputs, grads):
    tokens, breadth = grads.shape
    vmem = pltpu.VMEM
    tall, short = (BOTH, breadth), (ROWS + HEAD, breadth)

    def fetched(steps):
        return ((len(steps), tokens, BOTH), BF, vmem)

    def sems(steps):
        return pltpu.SemaphoreType.DMA((len(steps),))

    early = [((BOTH, breadth // 2), F32, vmem), ((3, *short), I16, vmem)]
    kept = [(tall, F32, pl.ANY)] * 3
    late = [((ROWS, breadth), F32, vmem)] + [(short, I16, vmem)] * 5
    both = vmem(tall, F32)

    def args(blocks, behind):
        return (inputs, pl.ANY), (held, vmem), (blocks, vmem), (behind, pl.ANY)

    keep4, away, held, ahead = partial_sums(
        first_kernel, ((inputs, pl.ANY), (grads, pl.ANY)), early + [(grads.shape, BF, vmem), fetched(EARLY)],
        [vmem((len(EARLY), tokens, BOTH), BF), both, sems(EARLY), sems(EARLY), pltpu.SemaphoreType.DMA], 3, "early")
    behind = yield keep4, away
    keep4, away, ahead = partial_sums(
        early_kernel, args(ahead, behind), early + [fetched(KEPT)], [both, sems(KEPT)], 2, "early")
    behind = yield keep4, away
    sums = [vmem((3, *tall), F32), sems(KEPT)]
    *keeps, ahead = partial_sums(
        lambda *refs: kept_kernel((KEPT, False), *refs), args(ahead, behind), kept + [fetched(KEPT)], sums + [sems(KEPT)], 3, "kept")
    behind = yield keeps
    *keeps, ahead = partial_sums(
        lambda *refs: kept_kernel((LATE, True), *refs), args(ahead, behind), kept + [fetched(LATE)], sums + [sems(LATE)], 3, "kept")
    behind = yield keeps
    keep0, *away, ahead = partial_sums(
        lambda *refs: late_kernel((LATE, False), *refs), args(ahead, behind), late + [fetched(LATE)], [both, sems(LATE)], 3, "late")
    behind = yield keep0, away
    keep0, *away = partial_sums(
        lambda *refs: late_kernel(None, *refs), args(ahead, behind), late, [both], 3, "late")
    yield keep0, away


ANYWHERE = "any"


def call_local(kernel, args, specs, outs, name, scratch=()):
    def spec(arg, cut):
        if cut == ANYWHERE:
            return pl.BlockSpec(memory_space=pl.ANY)
        block, index = cut or (arg.shape, (0,) * arg.ndim)
        return pl.BlockSpec(block, lambda i: index)

    result = pl.pallas_call(
        kernel,
        grid=(1,),
        in_specs=[spec(arg, cut) for arg, cut in zip(args, specs)],
        out_specs=[pl.BlockSpec(shape, lambda i, n=len(shape): (0,) * n) for shape, _ in outs],
        out_shape=[jax.ShapeDtypeStruct(*out) for out in outs],
        scratch_shapes=list(scratch),
        compiler_params=pltpu.CompilerParams(vmem_limit_bytes=16 << 20),
        cost_estimate=pl.CostEstimate(flops=10 * BOTH * 512, bytes_accessed=10 * BOTH * 512, transcendentals=0),
        name=name,
    )(*args)
    return result


def decode_pair(low, high):
    return jnp.concatenate([decode(low), decode(high)], axis=0)


def first_hop_kernel(keep, other, out):
    half = keep.shape[1]
    encode(keep[...] + decode_pair(other.at[:, :half], other.at[:, half:]), out)


def second_hop_kernel(keep, low, high, arrived, _, out, total):
    half = arrived.shape[1]
    total[...] = keep[...] + decode_pair(low, high)
    mine = pl.ds(pl.multiple_of(place()[2] * half, half), half)
    total[:, mine] += decode(arrived)
    encode(total[...], out)


def later_hop_kernel(keep, low, high, arrived, *rest):
    out = rest[-1]
    encode(keep[...] + decode_pair(low, high) + decode(arrived), out)


def own_kernel(keep, other, out):
    encode(keep[...] + decode(other), out)


def last_hop_kernel(keep, low, high, arrived, _, mine, other, total):
    core = place()[2]
    total[...] = keep[...] + decode_pair(low, high) + decode(arrived)
    encode(total[pl.ds(pl.multiple_of(core * ROWS, ROWS), ROWS), :], mine)
    encode(total[pl.ds(pl.multiple_of((1 - core) * ROWS, ROWS), ROWS), :], other)


def replica_sum(inputs, grads):
    breadth = grads.shape[1]
    tall, short = BOTH + HEAD, ROWS + HEAD

    def send(array, pairs):
        return lax.ppermute(array, "fsdp", pairs)

    def unit(n):
        return (None, short, breadth), (n, 0, 0)

    def first_hop(keep, other):
        return call_local(first_hop_kernel, (keep, other), (None, unit(0)), [((tall, breadth // 2), I16)], "hop1")[0]

    def later_hop(step, keep, others, arrived, after):
        if step == 2:
            others, cuts = (others, others), (unit(1), unit(2))
        else:
            others, cuts = others[2 * step - 6:2 * step - 4], (None, None)
        kernel = {2: second_hop_kernel, 3: later_hop_kernel, 4: last_hop_kernel}[step]
        outs = [((tall, breadth), I16)] if step < 4 else [((short, breadth), I16)] * 2
        scratch = [] if step == 3 else [pltpu.VMEM((BOTH, breadth), F32)]
        return call_local(kernel, (keep, *others, arrived, after), (None, *cuts, None, ANYWHERE), outs, "hop%d" % step, scratch)

    sums = all_sums(inputs, grads)
    keep4_a, away = next(sums)
    early_a = send(away, WITHIN)
    keep4_b, away = sums.send(away)
    early_b = send(away, WITHIN)
    ring_a = first_hop(keep4_a, early_a)
    ring_b = first_hop(keep4_b, early_b)
    kept_a = sums.send(ring_a)
    kept_b = sums.send(kept_a[0])
    ring_a, = later_hop(2, kept_a[0], early_a, send(ring_a, ALONG), kept_a[0])
    ring_b, = later_hop(2, kept_b[0], early_b, send(ring_b, ALONG), kept_b[0])
    keep0_a, away = sums.send(ring_a)
    late_a = [send(part, WITHIN) for part in away]
    keep0_b, away = sums.send(ring_b)
    late_b = [send(part, WITHIN) for part in away]
    own_a = call_local(own_kernel, (keep0_a, late_a[4]), (None, None), [((short, breadth), I16)], "own")[0]
    beside = send(own_a, BESIDE)
    ring_a, = later_hop(3, kept_a[1], late_a, send(ring_a, ALONG), own_a)
    ring_b, = later_hop(3, kept_b[1], late_b, send(ring_b, ALONG), own_a)
    mine_a, other_a = later_hop(4, kept_a[2], late_a, send(ring_a, ALONG), own_a)
    mine_b, other_b = later_hop(4, kept_b[2], late_b, send(ring_b, ALONG), own_a)
    parts = (
        late_b[4], beside, send(mine_a, ASLANT), send(other_a, ASLANT_ACROSS), send(mine_b, ALONG), send(other_b, ACROSS),
    )
    return keep0_b, parts


def spread(row, height):
    return jnp.concatenate([jnp.broadcast_to(row, (HEAD, row.shape[1])).astype(BF)] * (height // HEAD), axis=0)


def row_numbers(height, width):
    return lax.broadcasted_iota(jnp.int32, (height, width), 0).astype(F32).astype(BF)


def pick_kernel(kept, *refs):
    parts, (momentum, places, rows, rows_t, cols, cols_t, new_moment, payload, coef, sparse) = refs[:6], refs[6:]
    grad = kept[...]
    for part in parts:
        grad = grad + decode(part)
    moment = 0.9 * momentum[...] + grad
    coef[...] = right_product(left_product(rows, moment), cols_t)
    tile_rows, tile_cols = momentum.shape[0] // CH, momentum.shape[1] // CH
    group = 4
    tiles = tile_rows * tile_cols
    width = group * SLOTS
    numbers = row_numbers(group * CH, width)
    one, none = jnp.ones((), BF), jnp.zeros((), BF)
    for i in range(tile_rows):
        for h in range(tile_cols // group):
            first = i * tile_cols + h * group
            part = [places[first + n:first + n + 1, :] for n in range(group)]
            row_code = (jnp.concatenate(part, axis=1) >> 6).astype(F32)
            col_code = jnp.concatenate([(p & 63) + CH * n for n, p in enumerate(part)], axis=1).astype(F32)
            col_hot = jnp.where(numbers == spread(col_code, group * CH), one, none)
            row_hot = jnp.where(numbers[:CH] == spread(row_code, CH), one, none)
            block = coef[i * CH:(i + 1) * CH, h * group * CH:(h + 1) * group * CH]
            high, low = split(block)
            chosen = dot(jnp.concatenate([high, low], axis=0), col_hot)
            chosen = chosen[:CH] + chosen[CH:]
            value = jnp.sum(chosen * row_hot.astype(F32), axis=0, keepdims=True)
            for n in range(group):
                for r in range(payload.shape[0]):
                    payload[r, first + n:first + n + 1, :] = value[:, n * SLOTS:(n + 1) * SLOTS]
            sparse[i * CH:(i + 1) * CH, h * group * CH:(h + 1) * group * CH] = block * dot_nt(row_hot, col_hot)
    for r in range(payload.shape[0]):
        payload[r, tiles:, :] = places[...].astype(F32)
    new_moment[...] = moment - right_product(left_product(rows_t, sparse[...]), cols)


def decode_kernel(gathered, rows_t, cols, step_dir, total):
    reps = gathered.shape[0]
    tiles = gathered.shape[1] // 2
    tile_cols = total.shape[1] // CH
    numbers = row_numbers(CH, SLOTS)
    one, none = jnp.ones((), BF), jnp.zeros((), BF)
    parts = []
    for r in range(reps):
        high, low = split(gathered[r, :tiles, :])
        place = gathered[r, tiles:, :].astype(jnp.int32)
        parts.append([high.astype(F32), low.astype(F32), (place >> 6).astype(F32), (place & 63).astype(F32)])
    for pair in range(tiles // 2):
        blocks = []
        for t in (2 * pair, 2 * pair + 1):
            highs, lows, hots = [], [], []
            for r in range(reps):
                high, low, row_code, col_code = (spread(part[t:t + 1, :], CH) for part in parts[r])
                in_row = numbers == row_code
                highs.append(jnp.where(in_row, high, none))
                lows.append(jnp.where(in_row, low, none))
                hots.append(jnp.where(numbers == col_code, one, none))
            both = jnp.concatenate([jnp.concatenate(highs, axis=1), jnp.concatenate(lows, axis=1)], axis=0)
            out = dot_nt(both, jnp.concatenate(hots, axis=1))
            blocks.append(out[:CH] + out[CH:])
        i, j = (2 * pair) // tile_cols, (2 * pair) % tile_cols
        total[i * CH:(i + 1) * CH, j * CH:(j + 2) * CH] = jnp.concatenate(blocks, axis=1)
    decoded = right_product(left_product(rows_t, total[...]), cols)
    step_dir[...] = decoded * lax.rsqrt(decoded * decoded + 0.04)


def body(activations, out_grads, momentum, indices, counts):
    reps = lax.axis_size("rep")
    table = cosine_table(CH)
    rows = np.kron(np.eye(3), table)
    cols = np.kron(np.eye(4), table)
    rows, rows_t, cols, cols_t = (jnp.asarray(two_terms(m)) for m in (rows, rows.T, cols, cols.T))
    height, breadth = momentum.shape[1:]
    tiles = (height // CH) * (breadth // CH)
    live = lax.broadcasted_iota(jnp.int32, indices.shape[1:], 2) < counts[0]
    places = jnp.where(live, indices[0], -1).reshape(tiles, SLOTS)
    kept, parts = replica_sum(activations[0], out_grads[0])
    new_moment, payload = pl.pallas_call(
        pick_kernel,
        out_shape=[
            jax.ShapeDtypeStruct((height, breadth), F32),
            jax.ShapeDtypeStruct((reps, 2 * tiles, SLOTS), F32),
        ],
        scratch_shapes=[pltpu.VMEM((height, breadth), F32), pltpu.VMEM((height, breadth), F32)],
        compiler_params=pltpu.CompilerParams(vmem_limit_bytes=32 << 20),
        name="pick",
    )(kept, *parts, momentum[0], places, rows, rows_t, cols, cols_t)
    gathered = lax.all_to_all(payload, "rep", 0, 0)
    step_dir = pl.pallas_call(
        decode_kernel,
        out_shape=jax.ShapeDtypeStruct((height, breadth), F32),
        scratch_shapes=[pltpu.VMEM((height, breadth), F32)],
        compiler_params=pltpu.CompilerParams(vmem_limit_bytes=32 << 20),
        name="decode",
    )(gathered, rows_t, cols)
    return (new_moment[None], step_dir)


def solution(mesh):
    placed = (
        P("rep", "fsdp", None),
        P("rep", "fsdp", None),
        P("rep", "fsdp", None),
        P("rep", "fsdp", None, None),
        P("rep"),
    )
    return jax.shard_map(
        body,
        mesh=mesh,
        in_specs=placed,
        out_specs=(P("rep", "fsdp", None), P("fsdp", None)),
        check_vma=False,
    )
```

```python
import math

import jax
import jax.numpy as jnp
import numpy as np
from jax import lax
from jax.experimental import pallas as pl
from jax.experimental.pallas import tpu as pltpu
from jax.sharding import PartitionSpec as P

CH = 64
SLOTS = 128
BF = jnp.bfloat16
F32 = jnp.float32
I16 = jnp.int16
HEAD = 16
RINGS = 8
ROWS = 192
BOTH = 2 * ROWS


def cosine_table(side):
    freq = np.arange(side, dtype=np.float64)[:, None]
    place = np.arange(side, dtype=np.float64)[None, :]
    table = np.cos(math.pi * (2.0 * place + 1.0) * freq / (2.0 * side)) * math.sqrt(2.0 / side)
    return np.where(freq < 0.5, table * math.sqrt(0.5), table)


def two_terms(matrix):
    high = matrix.astype(np.float32).astype(BF)
    low = (matrix - high.astype(np.float64)).astype(np.float32).astype(BF)
    return np.stack([high, low])


def split(x):
    high = x.astype(BF)
    return high, (x - high.astype(F32)).astype(BF)


def dot(a, b):
    return jnp.dot(a, b, preferred_element_type=F32)


def dot_nt(a, b):
    return lax.dot_general(a, b, (((1,), (1,)), ((), ())), preferred_element_type=F32)


def left_product(table, x):
    high, low = split(x)
    height = table.shape[1]
    both = dot(jnp.concatenate([table[0], table[1]], axis=0), high)
    return both[:height] + (both[height:] + dot(table[0], low))


def right_product(x, table):
    width = table.shape[-1]
    height = x.shape[0]
    pieces = []
    for start in range(0, x.shape[1], width):
        high, low = split(x[:, start:start + width])
        both = dot(jnp.concatenate([high, low], axis=0), table[0])
        pieces.append(both[:height] + (both[height:] + dot(high, table[1])))
    return jnp.concatenate(pieces, axis=1)


def encode(x, out):
    top = jnp.max(jnp.abs(x), axis=0, keepdims=True)
    code = jnp.ceil(128.0 * jnp.log2(jnp.maximum(top, 1e-30))) + 1.0
    scale = 32767.0 * jnp.exp2(code * (-1.0 / 128.0))
    height = x.shape[0]
    out[:height, :] = jnp.round(x * scale).astype(jnp.int32).astype(I16)
    out[height:, :] = jnp.broadcast_to(code, (HEAD, x.shape[1])).astype(jnp.int32).astype(I16)


def decode(ref):
    height = ref.shape[0] - HEAD
    code = ref[height:, :].astype(jnp.int32).astype(F32)[:1, :]
    scale = jnp.exp2(code * (1.0 / 128.0)) * (1.0 / 32767.0)
    return ref[:height, :].astype(jnp.int32).astype(F32) * scale


def place():
    me = lax.axis_index("fsdp")
    return me // 4, lax.rem(me // 2, 2), lax.rem(me, 2)


def route(move):
    pairs = []
    for source in range(4 * RINGS):
        z, y, core = move(source // 4, (source // 2) % 2, source % 2)
        pairs.append((source, ((z % RINGS) * 2 + y) * 2 + core))
    return pairs


ALONG = route(lambda z, y, c: (z + 1 - 2 * c, y, c))
ACROSS = route(lambda z, y, c: (z + 1 - 2 * c, y, 1 - c))
ASLANT = route(lambda z, y, c: (z + 1 - 2 * c, 1 - y, c))
ASLANT_ACROSS = route(lambda z, y, c: (z + 1 - 2 * c, 1 - y, 1 - c))
BESIDE = route(lambda z, y, c: (z, 1 - y, c))
WITHIN = route(lambda z, y, c: (z, y, 1 - c))


def product(left, right):
    return lax.dot_general(left, right, (((0,), (0,)), ((), ())), preferred_element_type=F32)


EARLY = (4, -3)
LATE = (-2, -1)
KEPT = (3, 2, 1, 0)


def loads(steps, swap, inputs, blocks, sems):
    z, y, core = place()
    target = 1 - y if swap else y
    copies = []
    for n, step in enumerate(steps):
        block = lax.rem(z + step * (1 - 2 * core) + RINGS, RINGS) * 2 + target
        columns = pl.ds(pl.multiple_of(block * BOTH, BOTH), BOTH)
        copies.append(pltpu.make_async_copy(inputs.at[:, columns], blocks.at[n], sems.at[n]))
    return copies


def early_part(core, blocks, grads, keep4, away, both, ready=None):
    half = keep4.shape[1]
    both[...] = product(blocks[0], grads[...])
    keep4[...] = both[:, pl.ds(pl.multiple_of(core * half, half), half)]
    other = both[:, pl.ds(pl.multiple_of((1 - core) * half, half), half)]
    encode(other[:ROWS], away.at[0, :, :half])
    encode(other[ROWS:], away.at[0, :, half:])
    if ready is not None:
        ready.wait()
    total = product(blocks[1], grads[...])
    encode(total[:ROWS], away.at[1])
    encode(total[ROWS:], away.at[2])


def first_kernel(inputs, grads, keep4, away, kept_grads, ahead, blocks, both, sems, ahead_sems, grad_sem):
    whole = pltpu.make_async_copy(grads, kept_grads, grad_sem)
    mine = loads(EARLY, True, inputs, blocks, sems)
    more = loads(EARLY, False, inputs, ahead, ahead_sems)
    whole.start()
    mine[0].start()
    mine[1].start()
    whole.wait()
    mine[0].wait()
    for copy in more:
        copy.start()
    early_part(place()[2], blocks, kept_grads, keep4, away, both, mine[1])
    for copy in more:
        copy.wait()


def early_kernel(inputs, grads, blocks, _, keep4, away, ahead, both, sems):
    more = loads(KEPT, True, inputs, ahead, sems)
    for copy in more:
        copy.start()
    early_part(place()[2], blocks, grads, keep4, away, both)
    for copy in more:
        copy.wait()


def kept_kernel(then, inputs, grads, blocks, _, *refs):
    keeps, (keep0, away0, ahead, sums, out_sems, both, sems) = refs[:3], refs[3:]
    more = loads(*then, inputs, ahead, sems)
    for copy in more:
        copy.start()
    core = place()[2]
    both[...] = product(blocks[3], grads[...])
    keep0[...] = both[pl.ds(pl.multiple_of(core * ROWS, ROWS), ROWS), :]
    encode(both[pl.ds(pl.multiple_of((1 - core) * ROWS, ROWS), ROWS), :], away0)
    copies = []
    for n, keep in enumerate(keeps):
        sums[n] = product(blocks[n], grads[...])
        copies.append(pltpu.make_async_copy(sums.at[n], keep, out_sems.at[n]))
        copies[n].start()
    for copy in copies + more:
        copy.wait()


def late_kernel(then, inputs, grads, blocks, _, *refs):
    away, refs = refs[:4], refs[4:]
    more = loads(*then, inputs, *refs) if then else []
    for copy in more:
        copy.start()
    for n in range(2):
        total = product(blocks[n], grads[...])
        encode(total[:ROWS], away[2 * n])
        encode(total[ROWS:], away[2 * n + 1])
    for copy in more:
        copy.wait()


def partial_sums(kernel, args, outs, scratch, steps, name):
    tokens, breadth = args[1][0].shape
    return pl.pallas_call(
        kernel,
        in_specs=[pl.BlockSpec(memory_space=space) for _, space in args],
        out_specs=[pl.BlockSpec(memory_space=space) for _, _, space in outs],
        out_shape=[jax.ShapeDtypeStruct(shape, kind) for shape, kind, _ in outs],
        scratch_shapes=scratch,
        compiler_params=pltpu.CompilerParams(vmem_limit_bytes=46 << 20),
        cost_estimate=pl.CostEstimate(
            flops=steps * 6 * BOTH * tokens * breadth,
            bytes_accessed=steps * (2 * BOTH * tokens + 2 * BOTH * breadth),
            transcendentals=0,
        ),
        name=name,
    )(*(array for array, _ in args))


def all_sums(inputs, grads):
    tokens, breadth = grads.shape
    vmem = pltpu.VMEM
    tall, short = (BOTH, breadth), (ROWS + HEAD, breadth)

    def fetched(steps):
        return ((len(steps), tokens, BOTH), BF, vmem)

    def sems(steps):
        return pltpu.SemaphoreType.DMA((len(steps),))

    early = [((BOTH, breadth // 2), F32, vmem), ((3, *short), I16, vmem)]
    kept = [(tall, F32, pl.ANY)] * 3 + [((ROWS, breadth), F32, vmem), (short, I16, vmem)]
    late = [(short, I16, vmem)] * 4
    both = vmem(tall, F32)

    def args(blocks, behind):
        return (inputs, pl.ANY), (held, vmem), (blocks, vmem), (behind, pl.ANY)

    keep4, away, held, ahead = partial_sums(
        first_kernel, ((inputs, pl.ANY), (grads, pl.ANY)), early + [(grads.shape, BF, vmem), fetched(EARLY)],
        [vmem((len(EARLY), tokens, BOTH), BF), both, sems(EARLY), sems(EARLY), pltpu.SemaphoreType.DMA], 3, "early")
    behind = yield keep4, away
    keep4, away, ahead = partial_sums(
        early_kernel, args(ahead, behind), early + [fetched(KEPT)], [both, sems(KEPT)], 2, "early")
    behind = yield keep4, away
    sums = [vmem((3, *tall), F32), pltpu.SemaphoreType.DMA((3,)), both]
    *keeps, ahead = partial_sums(
        lambda *refs: kept_kernel((KEPT, False), *refs), args(ahead, behind), kept + [fetched(KEPT)], sums + [sems(KEPT)], 4, "kept")
    behind = yield keeps
    *keeps, ahead = partial_sums(
        lambda *refs: kept_kernel((LATE, True), *refs), args(ahead, behind), kept + [fetched(LATE)], sums + [sems(LATE)], 4, "kept")
    behind = yield keeps
    *away, ahead = partial_sums(
        lambda *refs: late_kernel((LATE, False), *refs), args(ahead, behind), late + [fetched(LATE)], [sems(LATE)], 2, "late")
    behind = yield away
    yield partial_sums(
        lambda *refs: late_kernel(None, *refs), args(ahead, behind), late, [], 2, "late")


ANYWHERE = "any"


def call_local(kernel, args, specs, outs, name, scratch=()):
    def spec(arg, cut):
        if cut == ANYWHERE:
            return pl.BlockSpec(memory_space=pl.ANY)
        block, index = cut or (arg.shape, (0,) * arg.ndim)
        return pl.BlockSpec(block, lambda i: index)

    result = pl.pallas_call(
        kernel,
        grid=(1,),
        in_specs=[spec(arg, cut) for arg, cut in zip(args, specs)],
        out_specs=[pl.BlockSpec(shape, lambda i, n=len(shape): (0,) * n) for shape, _ in outs],
        out_shape=[jax.ShapeDtypeStruct(*out) for out in outs],
        scratch_shapes=list(scratch),
        compiler_params=pltpu.CompilerParams(vmem_limit_bytes=16 << 20),
        cost_estimate=pl.CostEstimate(flops=10 * BOTH * 512, bytes_accessed=10 * BOTH * 512, transcendentals=0),
        name=name,
    )(*args)
    return result


def decode_pair(low, high):
    return jnp.concatenate([decode(low), decode(high)], axis=0)


def first_hop_kernel(keep, other, out):
    half = keep.shape[1]
    encode(keep[...] + decode_pair(other.at[:, :half], other.at[:, half:]), out)


def second_hop_kernel(keep, low, high, arrived, _, out, total):
    half = arrived.shape[1]
    total[...] = keep[...] + decode_pair(low, high)
    mine = pl.ds(pl.multiple_of(place()[2] * half, half), half)
    total[:, mine] += decode(arrived)
    encode(total[...], out)


def join_kernel(keep, low, high, out):
    out[...] = keep[...] + decode_pair(low, high)


def later_hop_kernel(joined, arrived, _, out):
    encode(joined[...] + decode(arrived), out)


def own_kernel(keep, other, out):
    encode(keep[...] + decode(other), out)


def last_hop_kernel(joined, arrived, _, mine, other, total):
    core = place()[2]
    total[...] = joined[...] + decode(arrived)
    encode(total[pl.ds(pl.multiple_of(core * ROWS, ROWS), ROWS), :], mine)
    encode(total[pl.ds(pl.multiple_of((1 - core) * ROWS, ROWS), ROWS), :], other)


def replica_sum(inputs, grads):
    breadth = grads.shape[1]
    tall, short = BOTH + HEAD, ROWS + HEAD

    def send(array, pairs):
        return lax.ppermute(array, "fsdp", pairs)

    def unit(n):
        return (None, short, breadth), (n, 0, 0)

    def first_hop(keep, other):
        return call_local(first_hop_kernel, (keep, other), (None, unit(0)), [((tall, breadth // 2), I16)], "hop1")[0]

    def second_hop(keep, other, arrived, after):
        return call_local(
            second_hop_kernel, (keep, other, other, arrived, after), (None, unit(1), unit(2), None, ANYWHERE),
            [((tall, breadth), I16)], "hop2", [pltpu.VMEM((BOTH, breadth), F32)])[0]

    def join(keep, low, high):
        return call_local(join_kernel, (keep, low, high), (None,) * 3, [((BOTH, breadth), F32)], "join")[0]

    def third_hop(joined, arrived, after):
        return call_local(
            later_hop_kernel, (joined, arrived, after), (None, None, ANYWHERE), [((tall, breadth), I16)], "hop3")[0]

    def last_hop(joined, arrived, after):
        return call_local(
            last_hop_kernel, (joined, arrived, after), (None, None, ANYWHERE),
            [((short, breadth), I16)] * 2, "hop4", [pltpu.VMEM((BOTH, breadth), F32)])

    sums = all_sums(inputs, grads)
    keep4_a, away = next(sums)
    early_a = send(away, WITHIN)
    keep4_b, away = sums.send(away)
    early_b = send(away, WITHIN)
    ring_a = first_hop(keep4_a, early_a)
    ring_b = first_hop(keep4_b, early_b)
    *kept_a, keep0_a, away0 = sums.send(ring_a)
    away0_a = send(away0, WITHIN)
    *kept_b, keep0_b, away0 = sums.send(kept_a[0])
    away0_b = send(away0, WITHIN)
    own_a = call_local(own_kernel, (keep0_a, away0_a), (None, None), [((short, breadth), I16)], "own")[0]
    beside = send(own_a, BESIDE)
    ring_a = second_hop(kept_a[0], early_a, send(ring_a, ALONG), kept_a[0])
    ring_b = second_hop(kept_b[0], early_b, send(ring_b, ALONG), own_a)
    late_a = [send(part, WITHIN) for part in sums.send(ring_a)]
    late_b = [send(part, WITHIN) for part in sums.send(ring_b)]
    ring_a = third_hop(join(kept_a[1], *late_a[:2]), send(ring_a, ALONG), own_a)
    ring_b = third_hop(join(kept_b[1], *late_b[:2]), send(ring_b, ALONG), away0_b)
    mine_a, other_a = last_hop(join(kept_a[2], *late_a[2:]), send(ring_a, ALONG), own_a)
    mine_b, other_b = last_hop(join(kept_b[2], *late_b[2:]), send(ring_b, ALONG), own_a)
    parts = (
        away0_b, beside, send(mine_a, ASLANT), send(other_a, ASLANT_ACROSS), send(mine_b, ALONG), send(other_b, ACROSS),
    )
    return keep0_b, parts, own_a


def spread(row, height):
    return jnp.concatenate([jnp.broadcast_to(row, (HEAD, row.shape[1])).astype(BF)] * (height // HEAD), axis=0)


def row_numbers(height, width):
    return lax.broadcasted_iota(jnp.int32, (height, width), 0).astype(F32).astype(BF)


GROUP = 4


def hot_kernel(places, _, col_hots, row_hots, mask):
    tile_cols = mask.shape[1] // CH
    numbers = row_numbers(GROUP * CH, GROUP * SLOTS)
    one, none = jnp.ones((), BF), jnp.zeros((), BF)
    for g in range(col_hots.shape[0]):
        part = [places[GROUP * g + n:GROUP * g + n + 1, :] for n in range(GROUP)]
        row_code = (jnp.concatenate(part, axis=1) >> 6).astype(F32)
        col_code = jnp.concatenate([(p & 63) + CH * n for n, p in enumerate(part)], axis=1).astype(F32)
        col_hots[g] = jnp.where(numbers == spread(col_code, GROUP * CH), one, none)
        row_hots[g] = jnp.where(numbers[:CH] == spread(row_code, CH), one, none)
        i, j = (GROUP * g) // tile_cols, (GROUP * g) % tile_cols
        mask[i * CH:(i + 1) * CH, j * CH:(j + GROUP) * CH] = dot_nt(row_hots[g], col_hots[g])


def pick_kernel(kept, *refs):
    parts, refs = refs[:6], refs[6:]
    momentum, places, col_hots, row_hots, mask, rows, rows_t, cols, cols_t, new_moment, payload, coef = refs
    grad = kept[...]
    for part in parts:
        grad = grad + decode(part)
    moment = 0.9 * momentum[...] + grad
    coef[...] = right_product(left_product(rows, moment), cols_t)
    tile_cols = momentum.shape[1] // CH
    for g in range(col_hots.shape[0]):
        i, j = (GROUP * g) // tile_cols, (GROUP * g) % tile_cols
        high, low = split(coef[i * CH:(i + 1) * CH, j * CH:(j + GROUP) * CH])
        chosen = dot(jnp.concatenate([high, low], axis=0), col_hots[g])
        chosen = chosen[:CH] + chosen[CH:]
        value = jnp.sum(chosen * row_hots[g].astype(F32), axis=0, keepdims=True)
        for n in range(GROUP):
            for r in range(payload.shape[0]):
                payload[r, GROUP * g + n:GROUP * g + n + 1, :] = value[:, n * SLOTS:(n + 1) * SLOTS]
    tiles = places.shape[0]
    for r in range(payload.shape[0]):
        payload[r, tiles:, :] = places[...].astype(F32)
    new_moment[...] = moment - right_product(left_product(rows_t, coef[...] * mask[...]), cols)


def decode_kernel(gathered, rows_t, cols, step_dir, total):
    reps = gathered.shape[0]
    tiles = gathered.shape[1] // 2
    tile_cols = total.shape[1] // CH
    numbers = row_numbers(CH, SLOTS)
    one, none = jnp.ones((), BF), jnp.zeros((), BF)
    parts = []
    for r in range(reps):
        high, low = split(gathered[r, :tiles, :])
        place = gathered[r, tiles:, :].astype(jnp.int32)
        parts.append([high.astype(F32), low.astype(F32), (place >> 6).astype(F32), (place & 63).astype(F32)])
    for pair in range(tiles // 2):
        blocks = []
        for t in (2 * pair, 2 * pair + 1):
            highs, lows, hots = [], [], []
            for r in range(reps):
                high, low, row_code, col_code = (spread(part[t:t + 1, :], CH) for part in parts[r])
                in_row = numbers == row_code
                highs.append(jnp.where(in_row, high, none))
                lows.append(jnp.where(in_row, low, none))
                hots.append(jnp.where(numbers == col_code, one, none))
            both = jnp.concatenate([jnp.concatenate(highs, axis=1), jnp.concatenate(lows, axis=1)], axis=0)
            out = dot_nt(both, jnp.concatenate(hots, axis=1))
            blocks.append(out[:CH] + out[CH:])
        i, j = (2 * pair) // tile_cols, (2 * pair) % tile_cols
        total[i * CH:(i + 1) * CH, j * CH:(j + 2) * CH] = jnp.concatenate(blocks, axis=1)
    decoded = right_product(left_product(rows_t, total[...]), cols)
    step_dir[...] = decoded * lax.rsqrt(decoded * decoded + 0.04)


def body(activations, out_grads, momentum, indices, counts):
    reps = lax.axis_size("rep")
    table = cosine_table(CH)
    rows = np.kron(np.eye(3), table)
    cols = np.kron(np.eye(4), table)
    rows, rows_t, cols, cols_t = (jnp.asarray(two_terms(m)) for m in (rows, rows.T, cols, cols.T))
    height, breadth = momentum.shape[1:]
    tiles = (height // CH) * (breadth // CH)
    live = lax.broadcasted_iota(jnp.int32, indices.shape[1:], 2) < counts[0]
    places = jnp.where(live, indices[0], -1).reshape(tiles, SLOTS)
    kept, parts, after = replica_sum(activations[0], out_grads[0])
    groups = tiles // GROUP
    hots = call_local(hot_kernel, (places, after), (None, ANYWHERE), [
        ((groups, GROUP * CH, GROUP * SLOTS), BF), ((groups, CH, GROUP * SLOTS), BF), ((height, breadth), F32),
    ], "hot")
    new_moment, payload = pl.pallas_call(
        pick_kernel,
        out_shape=[
            jax.ShapeDtypeStruct((height, breadth), F32),
            jax.ShapeDtypeStruct((reps, 2 * tiles, SLOTS), F32),
        ],
        scratch_shapes=[pltpu.VMEM((height, breadth), F32)],
        compiler_params=pltpu.CompilerParams(vmem_limit_bytes=32 << 20),
        name="pick",
    )(kept, *parts, momentum[0], places, *hots, rows, rows_t, cols, cols_t)
    gathered = lax.all_to_all(payload, "rep", 0, 0)
    step_dir = pl.pallas_call(
        decode_kernel,
        out_shape=jax.ShapeDtypeStruct((height, breadth), F32),
        scratch_shapes=[pltpu.VMEM((height, breadth), F32)],
        compiler_params=pltpu.CompilerParams(vmem_limit_bytes=32 << 20),
        name="decode",
    )(gathered, rows_t, cols)
    return (new_moment[None], step_dir)


def solution(mesh):
    placed = (
        P("rep", "fsdp", None),
        P("rep", "fsdp", None),
        P("rep", "fsdp", None),
        P("rep", "fsdp", None, None),
        P("rep"),
    )
    return jax.shard_map(
        body,
        mesh=mesh,
        in_specs=placed,
        out_specs=(P("rep", "fsdp", None), P("fsdp", None)),
        check_vma=False,
    )
```

```python
import math

import jax
import jax.numpy as jnp
import numpy as np
from jax import lax
from jax.experimental import pallas as pl
from jax.experimental.pallas import tpu as pltpu
from jax.sharding import PartitionSpec as P

CH = 64
SLOTS = 128
BF = jnp.bfloat16
F32 = jnp.float32
I16 = jnp.int16
HEAD = 16
RINGS = 8
ROWS = 192
BOTH = 2 * ROWS


def cosine_table(side):
    freq = np.arange(side, dtype=np.float64)[:, None]
    place = np.arange(side, dtype=np.float64)[None, :]
    table = np.cos(math.pi * (2.0 * place + 1.0) * freq / (2.0 * side)) * math.sqrt(2.0 / side)
    return np.where(freq < 0.5, table * math.sqrt(0.5), table)


def two_terms(matrix):
    high = matrix.astype(np.float32).astype(BF)
    low = (matrix - high.astype(np.float64)).astype(np.float32).astype(BF)
    return np.stack([high, low])


def split(x):
    high = x.astype(BF)
    return high, (x - high.astype(F32)).astype(BF)


def dot(a, b):
    return jnp.dot(a, b, preferred_element_type=F32)


def dot_nt(a, b):
    return lax.dot_general(a, b, (((1,), (1,)), ((), ())), preferred_element_type=F32)


def left_product(table, x):
    high, low = split(x)
    height = table.shape[1]
    both = dot(jnp.concatenate([table[0], table[1]], axis=0), high)
    return both[:height] + (both[height:] + dot(table[0], low))


def right_product(x, table):
    width = table.shape[-1]
    height = x.shape[0]
    pieces = []
    for start in range(0, x.shape[1], width):
        high, low = split(x[:, start:start + width])
        both = dot(jnp.concatenate([high, low], axis=0), table[0])
        pieces.append(both[:height] + (both[height:] + dot(high, table[1])))
    return jnp.concatenate(pieces, axis=1)


def encode(x, out):
    top = jnp.max(jnp.abs(x), axis=0, keepdims=True)
    code = jnp.ceil(128.0 * jnp.log2(jnp.maximum(top, 1e-30))) + 1.0
    scale = 32767.0 * jnp.exp2(code * (-1.0 / 128.0))
    height = x.shape[0]
    out[:height, :] = jnp.round(x * scale).astype(jnp.int32).astype(I16)
    out[height:, :] = jnp.broadcast_to(code, (HEAD, x.shape[1])).astype(jnp.int32).astype(I16)


def decode(ref):
    height = ref.shape[0] - HEAD
    code = ref[height:, :].astype(jnp.int32).astype(F32)[:1, :]
    scale = jnp.exp2(code * (1.0 / 128.0)) * (1.0 / 32767.0)
    return ref[:height, :].astype(jnp.int32).astype(F32) * scale


def place():
    me = lax.axis_index("fsdp")
    return me // 4, lax.rem(me // 2, 2), lax.rem(me, 2)


def route(move):
    pairs = []
    for source in range(4 * RINGS):
        z, y, core = move(source // 4, (source // 2) % 2, source % 2)
        pairs.append((source, ((z % RINGS) * 2 + y) * 2 + core))
    return pairs


ALONG = route(lambda z, y, c: (z + 1 - 2 * c, y, c))
ACROSS = route(lambda z, y, c: (z + 1 - 2 * c, y, 1 - c))
ASLANT = route(lambda z, y, c: (z + 1 - 2 * c, 1 - y, c))
ASLANT_ACROSS = route(lambda z, y, c: (z + 1 - 2 * c, 1 - y, 1 - c))
BESIDE = route(lambda z, y, c: (z, 1 - y, c))
WITHIN = route(lambda z, y, c: (z, y, 1 - c))


def product(left, right):
    return lax.dot_general(left, right, (((0,), (0,)), ((), ())), preferred_element_type=F32)


EARLY = (4, -3)
LATE = (-2, -1)
KEPT = (3, 2, 1)
OWN = (0,)


def loads(steps, swap, inputs, blocks, sems):
    z, y, core = place()
    target = 1 - y if swap else y
    copies = []
    for n, step in enumerate(steps):
        block = lax.rem(z + step * (1 - 2 * core) + RINGS, RINGS) * 2 + target
        columns = pl.ds(pl.multiple_of(block * BOTH, BOTH), BOTH)
        copies.append(pltpu.make_async_copy(inputs.at[:, columns], blocks.at[n], sems.at[n]))
    return copies


def early_part(core, blocks, grads, keep4, away, both, ready=None):
    half = keep4.shape[1]
    both[...] = product(blocks[0], grads[...])
    keep4[...] = both[:, pl.ds(pl.multiple_of(core * half, half), half)]
    other = both[:, pl.ds(pl.multiple_of((1 - core) * half, half), half)]
    encode(other[:ROWS], away.at[0, :, :half])
    encode(other[ROWS:], away.at[0, :, half:])
    if ready is not None:
        ready.wait()
    total = product(blocks[1], grads[...])
    encode(total[:ROWS], away.at[1])
    encode(total[ROWS:], away.at[2])


def first_kernel(inputs, grads, keep4, away, kept_grads, ahead, blocks, both, sems, ahead_sems, grad_sem):
    whole = pltpu.make_async_copy(grads, kept_grads, grad_sem)
    mine = loads(EARLY, True, inputs, blocks, sems)
    more = loads(EARLY, False, inputs, ahead, ahead_sems)
    whole.start()
    mine[0].start()
    mine[1].start()
    whole.wait()
    mine[0].wait()
    for copy in more:
        copy.start()
    early_part(place()[2], blocks, kept_grads, keep4, away, both, mine[1])
    for copy in more:
        copy.wait()


def early_kernel(inputs, grads, blocks, _, keep4, away, ahead, both, sems):
    more = loads(KEPT, True, inputs, ahead, sems)
    for copy in more:
        copy.start()
    early_part(place()[2], blocks, grads, keep4, away, both)
    for copy in more:
        copy.wait()


def kept_kernel(swap, then, inputs, grads, blocks, _, *refs):
    keeps, (keep0, away0, ahead, sums, out_sems, both, own, own_sem, sems) = refs[:3], refs[3:]
    mine, = loads(OWN, swap, inputs, own, own_sem)
    mine.start()
    more = loads(*then, inputs, ahead, sems)
    for copy in more:
        copy.start()
    copies = []
    for n, keep in enumerate(keeps):
        sums[n] = product(blocks[n], grads[...])
        copies.append(pltpu.make_async_copy(sums.at[n], keep, out_sems.at[n]))
        copies[n].start()
    core = place()[2]
    mine.wait()
    both[...] = product(own[0], grads[...])
    keep0[...] = both[pl.ds(pl.multiple_of(core * ROWS, ROWS), ROWS), :]
    encode(both[pl.ds(pl.multiple_of((1 - core) * ROWS, ROWS), ROWS), :], away0)
    for copy in copies + more:
        copy.wait()


def late_kernel(then, inputs, grads, blocks, _, *refs):
    away, refs = refs[:4], refs[4:]
    more = loads(*then, inputs, *refs) if then else []
    for copy in more:
        copy.start()
    for n in range(2):
        total = product(blocks[n], grads[...])
        encode(total[:ROWS], away[2 * n])
        encode(total[ROWS:], away[2 * n + 1])
    for copy in more:
        copy.wait()


def partial_sums(kernel, args, outs, scratch, steps, name):
    tokens, breadth = args[1][0].shape
    return pl.pallas_call(
        kernel,
        in_specs=[pl.BlockSpec(memory_space=space) for _, space in args],
        out_specs=[pl.BlockSpec(memory_space=space) for _, _, space in outs],
        out_shape=[jax.ShapeDtypeStruct(shape, kind) for shape, kind, _ in outs],
        scratch_shapes=scratch,
        compiler_params=pltpu.CompilerParams(vmem_limit_bytes=46 << 20),
        cost_estimate=pl.CostEstimate(
            flops=steps * 6 * BOTH * tokens * breadth,
            bytes_accessed=steps * (2 * BOTH * tokens + 2 * BOTH * breadth),
            transcendentals=0,
        ),
        name=name,
    )(*(array for array, _ in args))


def all_sums(inputs, grads):
    tokens, breadth = grads.shape
    vmem = pltpu.VMEM
    tall, short = (BOTH, breadth), (ROWS + HEAD, breadth)

    def fetched(steps):
        return ((len(steps), tokens, BOTH), BF, vmem)

    def sems(steps):
        return pltpu.SemaphoreType.DMA((len(steps),))

    early = [((BOTH, breadth // 2), F32, vmem), ((3, *short), I16, vmem)]
    kept = [(tall, F32, pl.ANY)] * 3 + [((ROWS, breadth), F32, vmem), (short, I16, vmem)]
    late = [(short, I16, vmem)] * 4
    both = vmem(tall, F32)

    def args(blocks, behind):
        return (inputs, pl.ANY), (held, vmem), (blocks, vmem), (behind, pl.ANY)

    keep4, away, held, ahead = partial_sums(
        first_kernel, ((inputs, pl.ANY), (grads, pl.ANY)), early + [(grads.shape, BF, vmem), fetched(EARLY)],
        [vmem((len(EARLY), tokens, BOTH), BF), both, sems(EARLY), sems(EARLY), pltpu.SemaphoreType.DMA], 3, "early")
    behind = yield keep4, away
    keep4, away, ahead = partial_sums(
        early_kernel, args(ahead, behind), early + [fetched(KEPT)], [both, sems(KEPT)], 2, "early")
    behind = yield keep4, away
    sums = [vmem((3, *tall), F32), sems(KEPT), both, vmem((1, tokens, BOTH), BF), sems(OWN)]
    *keeps, ahead = partial_sums(
        lambda *refs: kept_kernel(True, (KEPT, False), *refs), args(ahead, behind), kept + [fetched(KEPT)], sums + [sems(KEPT)], 4, "kept")
    behind = yield keeps
    *keeps, ahead = partial_sums(
        lambda *refs: kept_kernel(False, (LATE, True), *refs), args(ahead, behind), kept + [fetched(LATE)], sums + [sems(LATE)], 4, "kept")
    behind = yield keeps
    *away, ahead = partial_sums(
        lambda *refs: late_kernel((LATE, False), *refs), args(ahead, behind), late + [fetched(LATE)], [sems(LATE)], 2, "late")
    behind = yield away
    yield partial_sums(
        lambda *refs: late_kernel(None, *refs), args(ahead, behind), late, [], 2, "late")


ANYWHERE = "any"


def call_local(kernel, args, specs, outs, name, scratch=()):
    def spec(arg, cut):
        if cut == ANYWHERE:
            return pl.BlockSpec(memory_space=pl.ANY)
        block, index = cut or (arg.shape, (0,) * arg.ndim)
        return pl.BlockSpec(block, lambda i: index)

    result = pl.pallas_call(
        kernel,
        grid=(1,),
        in_specs=[spec(arg, cut) for arg, cut in zip(args, specs)],
        out_specs=[pl.BlockSpec(shape, lambda i, n=len(shape): (0,) * n) for shape, _ in outs],
        out_shape=[jax.ShapeDtypeStruct(*out) for out in outs],
        scratch_shapes=list(scratch),
        compiler_params=pltpu.CompilerParams(vmem_limit_bytes=16 << 20),
        cost_estimate=pl.CostEstimate(flops=10 * BOTH * 512, bytes_accessed=10 * BOTH * 512, transcendentals=0),
        name=name,
    )(*args)
    return result


def decode_pair(low, high):
    return jnp.concatenate([decode(low), decode(high)], axis=0)


def first_hop_kernel(keep, other, _, out):
    half = keep.shape[1]
    encode(keep[...] + decode_pair(other.at[:, :half], other.at[:, half:]), out)


def second_hop_kernel(keep, low, high, arrived, _, out, total):
    half = arrived.shape[1]
    total[...] = keep[...] + decode_pair(low, high)
    mine = pl.ds(pl.multiple_of(place()[2] * half, half), half)
    total[:, mine] += decode(arrived)
    encode(total[...], out)


def join_kernel(keep, low, high, out):
    out[...] = keep[...] + decode_pair(low, high)


def later_hop_kernel(joined, arrived, _, out):
    encode(joined[...] + decode(arrived), out)


def own_kernel(keep, other, out):
    encode(keep[...] + decode(other), out)


def last_hop_kernel(joined, arrived, _, mine, other, total):
    core = place()[2]
    total[...] = joined[...] + decode(arrived)
    encode(total[pl.ds(pl.multiple_of(core * ROWS, ROWS), ROWS), :], mine)
    encode(total[pl.ds(pl.multiple_of((1 - core) * ROWS, ROWS), ROWS), :], other)


def replica_sum(inputs, grads):
    breadth = grads.shape[1]
    tall, short = BOTH + HEAD, ROWS + HEAD

    def send(array, pairs):
        return lax.ppermute(array, "fsdp", pairs)

    def unit(n):
        return (None, short, breadth), (n, 0, 0)

    def first_hop(keep, other, after):
        return call_local(first_hop_kernel, (keep, other, after), (None, unit(0), ANYWHERE), [((tall, breadth // 2), I16)], "hop1")[0]

    def second_hop(keep, other, arrived, after):
        return call_local(
            second_hop_kernel, (keep, other, other, arrived, after), (None, unit(1), unit(2), None, ANYWHERE),
            [((tall, breadth), I16)], "hop2", [pltpu.VMEM((BOTH, breadth), F32)])[0]

    def join(keep, low, high):
        return call_local(join_kernel, (keep, low, high), (None,) * 3, [((BOTH, breadth), F32)], "join")[0]

    def third_hop(joined, arrived, after):
        return call_local(
            later_hop_kernel, (joined, arrived, after), (None, None, ANYWHERE), [((tall, breadth), I16)], "hop3")[0]

    def last_hop(joined, arrived, after):
        return call_local(
            last_hop_kernel, (joined, arrived, after), (None, None, ANYWHERE),
            [((short, breadth), I16)] * 2, "hop4", [pltpu.VMEM((BOTH, breadth), F32)])

    sums = all_sums(inputs, grads)
    keep4_a, away = next(sums)
    early_a = send(away, WITHIN)
    keep4_b, away = sums.send(away)
    early_b = send(away, WITHIN)
    ring_a = first_hop(keep4_a, early_a, keep4_a)
    ring_b = first_hop(keep4_b, early_b, ring_a)
    *kept_a, keep0_a, away0 = sums.send(ring_b)
    away0_a = send(away0, WITHIN)
    *kept_b, keep0_b, away0 = sums.send(kept_a[0])
    away0_b = send(away0, WITHIN)
    own_a = call_local(own_kernel, (keep0_a, away0_a), (None, None), [((short, breadth), I16)], "own")[0]
    beside = send(own_a, BESIDE)
    ring_a = second_hop(kept_a[0], early_a, send(ring_a, ALONG), kept_a[0])
    ring_b = second_hop(kept_b[0], early_b, send(ring_b, ALONG), own_a)
    late_a = [send(part, WITHIN) for part in sums.send(ring_a)]
    late_b = [send(part, WITHIN) for part in sums.send(ring_b)]
    ring_a = third_hop(join(kept_a[1], *late_a[:2]), send(ring_a, ALONG), own_a)
    ring_b = third_hop(join(kept_b[1], *late_b[:2]), send(ring_b, ALONG), away0_b)
    mine_a, other_a = last_hop(join(kept_a[2], *late_a[2:]), send(ring_a, ALONG), own_a)
    mine_b, other_b = last_hop(join(kept_b[2], *late_b[2:]), send(ring_b, ALONG), own_a)
    parts = (
        away0_b, beside, send(mine_a, ASLANT), send(other_a, ASLANT_ACROSS), send(mine_b, ALONG), send(other_b, ACROSS),
    )
    return keep0_b, parts, own_a


def spread(row, height):
    return jnp.concatenate([jnp.broadcast_to(row, (HEAD, row.shape[1])).astype(BF)] * (height // HEAD), axis=0)


def row_numbers(height, width):
    return lax.broadcasted_iota(jnp.int32, (height, width), 0).astype(F32).astype(BF)


GROUP = 4


def hot_kernel(places, _, col_hots, row_hots, mask):
    tile_cols = mask.shape[1] // CH
    numbers = row_numbers(GROUP * CH, GROUP * SLOTS)
    one, none = jnp.ones((), BF), jnp.zeros((), BF)
    for g in range(col_hots.shape[0]):
        part = [places[GROUP * g + n:GROUP * g + n + 1, :] for n in range(GROUP)]
        row_code = (jnp.concatenate(part, axis=1) >> 6).astype(F32)
        col_code = jnp.concatenate([(p & 63) + CH * n for n, p in enumerate(part)], axis=1).astype(F32)
        col_hots[g] = jnp.where(numbers == spread(col_code, GROUP * CH), one, none)
        row_hots[g] = jnp.where(numbers[:CH] == spread(row_code, CH), one, none)
        i, j = (GROUP * g) // tile_cols, (GROUP * g) % tile_cols
        mask[i * CH:(i + 1) * CH, j * CH:(j + GROUP) * CH] = dot_nt(row_hots[g], col_hots[g])


def pick_kernel(kept, *refs):
    parts, refs = refs[:6], refs[6:]
    momentum, places, col_hots, row_hots, mask, rows, rows_t, cols, cols_t, new_moment, payload, coef = refs
    grad = kept[...]
    for part in parts:
        grad = grad + decode(part)
    moment = 0.9 * momentum[...] + grad
    coef[...] = right_product(left_product(rows, moment), cols_t)
    tile_cols = momentum.shape[1] // CH
    for g in range(col_hots.shape[0]):
        i, j = (GROUP * g) // tile_cols, (GROUP * g) % tile_cols
        high, low = split(coef[i * CH:(i + 1) * CH, j * CH:(j + GROUP) * CH])
        chosen = dot(jnp.concatenate([high, low], axis=0), col_hots[g])
        chosen = chosen[:CH] + chosen[CH:]
        value = jnp.sum(chosen * row_hots[g].astype(F32), axis=0, keepdims=True)
        for n in range(GROUP):
            for r in range(payload.shape[0]):
                payload[r, GROUP * g + n:GROUP * g + n + 1, :] = value[:, n * SLOTS:(n + 1) * SLOTS]
    tiles = places.shape[0]
    for r in range(payload.shape[0]):
        payload[r, tiles:, :] = places[...].astype(F32)
    new_moment[...] = moment - right_product(left_product(rows_t, coef[...] * mask[...]), cols)


def decode_kernel(gathered, rows_t, cols, step_dir, total):
    reps = gathered.shape[0]
    tiles = gathered.shape[1] // 2
    tile_cols = total.shape[1] // CH
    numbers = row_numbers(CH, SLOTS)
    one, none = jnp.ones((), BF), jnp.zeros((), BF)
    parts = []
    for r in range(reps):
        high, low = split(gathered[r, :tiles, :])
        place = gathered[r, tiles:, :].astype(jnp.int32)
        parts.append([high.astype(F32), low.astype(F32), (place >> 6).astype(F32), (place & 63).astype(F32)])
    for pair in range(tiles // 2):
        blocks = []
        for t in (2 * pair, 2 * pair + 1):
            highs, lows, hots = [], [], []
            for r in range(reps):
                high, low, row_code, col_code = (spread(part[t:t + 1, :], CH) for part in parts[r])
                in_row = numbers == row_code
                highs.append(jnp.where(in_row, high, none))
                lows.append(jnp.where(in_row, low, none))
                hots.append(jnp.where(numbers == col_code, one, none))
            both = jnp.concatenate([jnp.concatenate(highs, axis=1), jnp.concatenate(lows, axis=1)], axis=0)
            out = dot_nt(both, jnp.concatenate(hots, axis=1))
            blocks.append(out[:CH] + out[CH:])
        i, j = (2 * pair) // tile_cols, (2 * pair) % tile_cols
        total[i * CH:(i + 1) * CH, j * CH:(j + 2) * CH] = jnp.concatenate(blocks, axis=1)
    decoded = right_product(left_product(rows_t, total[...]), cols)
    step_dir[...] = decoded * lax.rsqrt(decoded * decoded + 0.04)


def body(activations, out_grads, momentum, indices, counts):
    reps = lax.axis_size("rep")
    table = cosine_table(CH)
    rows = np.kron(np.eye(3), table)
    cols = np.kron(np.eye(4), table)
    rows, rows_t, cols, cols_t = (jnp.asarray(two_terms(m)) for m in (rows, rows.T, cols, cols.T))
    height, breadth = momentum.shape[1:]
    tiles = (height // CH) * (breadth // CH)
    live = lax.broadcasted_iota(jnp.int32, indices.shape[1:], 2) < counts[0]
    places = jnp.where(live, indices[0], -1).reshape(tiles, SLOTS)
    kept, parts, after = replica_sum(activations[0], out_grads[0])
    groups = tiles // GROUP
    hots = call_local(hot_kernel, (places, after), (None, ANYWHERE), [
        ((groups, GROUP * CH, GROUP * SLOTS), BF), ((groups, CH, GROUP * SLOTS), BF), ((height, breadth), F32),
    ], "hot")
    new_moment, payload = pl.pallas_call(
        pick_kernel,
        out_shape=[
            jax.ShapeDtypeStruct((height, breadth), F32),
            jax.ShapeDtypeStruct((reps, 2 * tiles, SLOTS), F32),
        ],
        scratch_shapes=[pltpu.VMEM((height, breadth), F32)],
        compiler_params=pltpu.CompilerParams(vmem_limit_bytes=32 << 20),
        name="pick",
    )(kept, *parts, momentum[0], places, *hots, rows, rows_t, cols, cols_t)
    gathered = lax.all_to_all(payload, "rep", 0, 0)
    step_dir = pl.pallas_call(
        decode_kernel,
        out_shape=jax.ShapeDtypeStruct((height, breadth), F32),
        scratch_shapes=[pltpu.VMEM((height, breadth), F32)],
        compiler_params=pltpu.CompilerParams(vmem_limit_bytes=32 << 20),
        name="decode",
    )(gathered, rows_t, cols)
    return (new_moment[None], step_dir)


def solution(mesh):
    placed = (
        P("rep", "fsdp", None),
        P("rep", "fsdp", None),
        P("rep", "fsdp", None),
        P("rep", "fsdp", None, None),
        P("rep"),
    )
    return jax.shard_map(
        body,
        mesh=mesh,
        in_specs=placed,
        out_specs=(P("rep", "fsdp", None), P("fsdp", None)),
        check_vma=False,
    )
```

```python
import math

import jax
import jax.numpy as jnp
import numpy as np
from jax import lax
from jax.experimental import pallas as pl
from jax.experimental.pallas import tpu as pltpu
from jax.sharding import PartitionSpec as P

CH = 64
SLOTS = 128
BF = jnp.bfloat16
F32 = jnp.float32
I16 = jnp.int16
HEAD = 16
RINGS = 8
ROWS = 192
BOTH = 2 * ROWS


def cosine_table(side):
    freq = np.arange(side, dtype=np.float64)[:, None]
    place = np.arange(side, dtype=np.float64)[None, :]
    table = np.cos(math.pi * (2.0 * place + 1.0) * freq / (2.0 * side)) * math.sqrt(2.0 / side)
    return np.where(freq < 0.5, table * math.sqrt(0.5), table)


def two_terms(matrix):
    high = matrix.astype(np.float32).astype(BF)
    low = (matrix - high.astype(np.float64)).astype(np.float32).astype(BF)
    return np.stack([high, low])


def split(x):
    high = x.astype(BF)
    return high, (x - high.astype(F32)).astype(BF)


def dot(a, b):
    return jnp.dot(a, b, preferred_element_type=F32)


def dot_nt(a, b):
    return lax.dot_general(a, b, (((1,), (1,)), ((), ())), preferred_element_type=F32)


def left_product(table, x):
    high, low = split(x)
    height = table.shape[1]
    both = dot(jnp.concatenate([table[0], table[1]], axis=0), high)
    return both[:height] + (both[height:] + dot(table[0], low))


def right_product(x, table):
    width = table.shape[-1]
    height = x.shape[0]
    pieces = []
    for start in range(0, x.shape[1], width):
        high, low = split(x[:, start:start + width])
        both = dot(jnp.concatenate([high, low], axis=0), table[0])
        pieces.append(both[:height] + (both[height:] + dot(high, table[1])))
    return jnp.concatenate(pieces, axis=1)


def encode(x, out):
    top = jnp.max(jnp.abs(x), axis=0, keepdims=True)
    code = jnp.ceil(128.0 * jnp.log2(jnp.maximum(top, 1e-30))) + 1.0
    scale = 32767.0 * jnp.exp2(code * (-1.0 / 128.0))
    height = x.shape[0]
    out[:height, :] = jnp.round(x * scale).astype(jnp.int32).astype(I16)
    out[height:, :] = jnp.broadcast_to(code, (HEAD, x.shape[1])).astype(jnp.int32).astype(I16)


def decode(ref):
    height = ref.shape[0] - HEAD
    code = ref[height:, :].astype(jnp.int32).astype(F32)[:1, :]
    scale = jnp.exp2(code * (1.0 / 128.0)) * (1.0 / 32767.0)
    return ref[:height, :].astype(jnp.int32).astype(F32) * scale


def place():
    me = lax.axis_index("fsdp")
    return me // 4, lax.rem(me // 2, 2), lax.rem(me, 2)


def route(move):
    pairs = []
    for source in range(4 * RINGS):
        z, y, core = move(source // 4, (source // 2) % 2, source % 2)
        pairs.append((source, ((z % RINGS) * 2 + y) * 2 + core))
    return pairs


ALONG = route(lambda z, y, c: (z + 1 - 2 * c, y, c))
ACROSS = route(lambda z, y, c: (z + 1 - 2 * c, y, 1 - c))
ASLANT = route(lambda z, y, c: (z + 1 - 2 * c, 1 - y, c))
ASLANT_ACROSS = route(lambda z, y, c: (z + 1 - 2 * c, 1 - y, 1 - c))
BESIDE = route(lambda z, y, c: (z, 1 - y, c))
WITHIN = route(lambda z, y, c: (z, y, 1 - c))


def product(left, right):
    return lax.dot_general(left, right, (((0,), (0,)), ((), ())), preferred_element_type=F32)


EARLY = (4, -3)
LATE = (-2, -1, 0)
KEPT = (3, 2, 1)


def loads(steps, swap, inputs, blocks, sems):
    z, y, core = place()
    target = 1 - y if swap else y
    copies = []
    for n, step in enumerate(steps):
        block = lax.rem(z + step * (1 - 2 * core) + RINGS, RINGS) * 2 + target
        columns = pl.ds(pl.multiple_of(block * BOTH, BOTH), BOTH)
        copies.append(pltpu.make_async_copy(inputs.at[:, columns], blocks.at[n], sems.at[n]))
    return copies


def early_part(core, blocks, grads, keep4, away, both, ready=None):
    half = keep4.shape[1]
    both[...] = product(blocks[0], grads[...])
    keep4[...] = both[:, pl.ds(pl.multiple_of(core * half, half), half)]
    other = both[:, pl.ds(pl.multiple_of((1 - core) * half, half), half)]
    encode(other[:ROWS], away.at[0, :, :half])
    encode(other[ROWS:], away.at[0, :, half:])
    if ready is not None:
        ready.wait()
    total = product(blocks[1], grads[...])
    encode(total[:ROWS], away.at[1])
    encode(total[ROWS:], away.at[2])


def first_kernel(inputs, grads, keep4, away, kept_grads, ahead, blocks, both, sems, ahead_sems, grad_sem):
    whole = pltpu.make_async_copy(grads, kept_grads, grad_sem)
    mine = loads(EARLY, True, inputs, blocks, sems)
    more = loads(EARLY, False, inputs, ahead, ahead_sems)
    whole.start()
    mine[0].start()
    mine[1].start()
    whole.wait()
    mine[0].wait()
    for copy in more:
        copy.start()
    early_part(place()[2], blocks, kept_grads, keep4, away, both, mine[1])
    for copy in more:
        copy.wait()


def early_kernel(inputs, grads, blocks, _, keep4, away, ahead, both, sems):
    more = loads(KEPT, True, inputs, ahead, sems)
    for copy in more:
        copy.start()
    early_part(place()[2], blocks, grads, keep4, away, both)
    for copy in more:
        copy.wait()


def kept_kernel(then, inputs, grads, blocks, _, *refs):
    keeps, (ahead, sums, out_sems, sems) = refs[:3], refs[3:]
    more = loads(*then, inputs, ahead, sems)
    for copy in more:
        copy.start()
    copies = []
    for n, keep in enumerate(keeps):
        sums[n] = product(blocks[n], grads[...])
        copies.append(pltpu.make_async_copy(sums.at[n], keep, out_sems.at[n]))
        copies[n].start()
    for copy in copies + more:
        copy.wait()


def late_kernel(then, inputs, grads, blocks, _, keep0, *refs):
    away, refs = refs[:5], refs[5:]
    more = loads(*then, inputs, refs[0], refs[2]) if then else []
    both = refs[1] if then else refs[0]
    for copy in more:
        copy.start()
    core = place()[2]
    for n in range(2):
        total = product(blocks[n], grads[...])
        encode(total[:ROWS], away[2 * n])
        encode(total[ROWS:], away[2 * n + 1])
    both[...] = product(blocks[2], grads[...])
    keep0[...] = both[pl.ds(pl.multiple_of(core * ROWS, ROWS), ROWS), :]
    encode(both[pl.ds(pl.multiple_of((1 - core) * ROWS, ROWS), ROWS), :], away[4])
    for copy in more:
        copy.wait()


def partial_sums(kernel, args, outs, scratch, steps, name):
    tokens, breadth = args[1][0].shape
    return pl.pallas_call(
        kernel,
        in_specs=[pl.BlockSpec(memory_space=space) for _, space in args],
        out_specs=[pl.BlockSpec(memory_space=space) for _, _, space in outs],
        out_shape=[jax.ShapeDtypeStruct(shape, kind) for shape, kind, _ in outs],
        scratch_shapes=scratch,
        compiler_params=pltpu.CompilerParams(vmem_limit_bytes=46 << 20),
        cost_estimate=pl.CostEstimate(
            flops=steps * 6 * BOTH * tokens * breadth,
            bytes_accessed=steps * (2 * BOTH * tokens + 2 * BOTH * breadth),
            transcendentals=0,
        ),
        name=name,
    )(*(array for array, _ in args))


def all_sums(inputs, grads):
    tokens, breadth = grads.shape
    vmem = pltpu.VMEM
    tall, short = (BOTH, breadth), (ROWS + HEAD, breadth)

    def fetched(steps):
        return ((len(steps), tokens, BOTH), BF, vmem)

    def sems(steps):
        return pltpu.SemaphoreType.DMA((len(steps),))

    early = [((BOTH, breadth // 2), F32, vmem), ((3, *short), I16, vmem)]
    kept = [(tall, F32, pl.ANY)] * 3
    late = [((ROWS, breadth), F32, vmem)] + [(short, I16, vmem)] * 5
    both = vmem(tall, F32)

    def args(blocks, behind):
        return (inputs, pl.ANY), (held, vmem), (blocks, vmem), (behind, pl.ANY)

    keep4, away, held, ahead = partial_sums(
        first_kernel, ((inputs, pl.ANY), (grads, pl.ANY)), early + [(grads.shape, BF, vmem), fetched(EARLY)],
        [vmem((len(EARLY), tokens, BOTH), BF), both, sems(EARLY), sems(EARLY), pltpu.SemaphoreType.DMA], 3, "early")
    behind = yield keep4, away
    keep4, away, ahead = partial_sums(
        early_kernel, args(ahead, behind), early + [fetched(KEPT)], [both, sems(KEPT)], 2, "early")
    behind = yield keep4, away
    sums = [vmem((3, *tall), F32), sems(KEPT)]
    *keeps, ahead = partial_sums(
        lambda *refs: kept_kernel((KEPT, False), *refs), args(ahead, behind), kept + [fetched(KEPT)], sums + [sems(KEPT)], 3, "kept")
    behind = yield keeps
    *keeps, ahead = partial_sums(
        lambda *refs: kept_kernel((LATE, True), *refs), args(ahead, behind), kept + [fetched(LATE)], sums + [sems(LATE)], 3, "kept")
    behind = yield keeps
    keep0, *away, ahead = partial_sums(
        lambda *refs: late_kernel((LATE, False), *refs), args(ahead, behind), late + [fetched(LATE)], [both, sems(LATE)], 3, "late")
    behind = yield keep0, away
    keep0, *away = partial_sums(
        lambda *refs: late_kernel(None, *refs), args(ahead, behind), late, [both], 3, "late")
    yield keep0, away


ANYWHERE = "any"


def call_local(kernel, args, specs, outs, name, scratch=()):
    def spec(arg, cut):
        if cut == ANYWHERE:
            return pl.BlockSpec(memory_space=pl.ANY)
        block, index = cut or (arg.shape, (0,) * arg.ndim)
        return pl.BlockSpec(block, lambda i: index)

    result = pl.pallas_call(
        kernel,
        grid=(1,),
        in_specs=[spec(arg, cut) for arg, cut in zip(args, specs)],
        out_specs=[pl.BlockSpec(shape, lambda i, n=len(shape): (0,) * n) for shape, _ in outs],
        out_shape=[jax.ShapeDtypeStruct(*out) for out in outs],
        scratch_shapes=list(scratch),
        compiler_params=pltpu.CompilerParams(vmem_limit_bytes=16 << 20),
        cost_estimate=pl.CostEstimate(flops=10 * BOTH * 512, bytes_accessed=10 * BOTH * 512, transcendentals=0),
        name=name,
    )(*args)
    return result


def decode_pair(low, high):
    return jnp.concatenate([decode(low), decode(high)], axis=0)


def first_hop_kernel(keep, other, out):
    half = keep.shape[1]
    encode(keep[...] + decode_pair(other.at[:, :half], other.at[:, half:]), out)


def second_hop_kernel(keep, low, high, arrived, _, out, total):
    half = arrived.shape[1]
    total[...] = keep[...] + decode_pair(low, high)
    mine = pl.ds(pl.multiple_of(place()[2] * half, half), half)
    total[:, mine] += decode(arrived)
    encode(total[...], out)


def later_hop_kernel(keep, low, high, arrived, *rest):
    out = rest[-1]
    encode(keep[...] + decode_pair(low, high) + decode(arrived), out)


def own_kernel(keep, other, out):
    encode(keep[...] + decode(other), out)


def last_hop_kernel(keep, low, high, arrived, _, mine, other, total):
    core = place()[2]
    total[...] = keep[...] + decode_pair(low, high) + decode(arrived)
    encode(total[pl.ds(pl.multiple_of(core * ROWS, ROWS), ROWS), :], mine)
    encode(total[pl.ds(pl.multiple_of((1 - core) * ROWS, ROWS), ROWS), :], other)


def replica_sum(inputs, grads):
    breadth = grads.shape[1]
    tall, short = BOTH + HEAD, ROWS + HEAD

    def send(array, pairs):
        return lax.ppermute(array, "fsdp", pairs)

    def unit(n):
        return (None, short, breadth), (n, 0, 0)

    def first_hop(keep, other):
        return call_local(first_hop_kernel, (keep, other), (None, unit(0)), [((tall, breadth // 2), I16)], "hop1")[0]

    def later_hop(step, keep, others, arrived, after):
        if step == 2:
            others, cuts = (others, others), (unit(1), unit(2))
        else:
            others, cuts = others[2 * step - 6:2 * step - 4], (None, None)
        kernel = {2: second_hop_kernel, 3: later_hop_kernel, 4: last_hop_kernel}[step]
        outs = [((tall, breadth), I16)] if step < 4 else [((short, breadth), I16)] * 2
        scratch = [] if step == 3 else [pltpu.VMEM((BOTH, breadth), F32)]
        return call_local(kernel, (keep, *others, arrived, after), (None, *cuts, None, ANYWHERE), outs, "hop%d" % step, scratch)

    sums = all_sums(inputs, grads)
    keep4_a, away = next(sums)
    early_a = send(away, WITHIN)
    keep4_b, away = sums.send(away)
    early_b = send(away, WITHIN)
    ring_a = first_hop(keep4_a, early_a)
    ring_b = first_hop(keep4_b, early_b)
    kept_a = sums.send(ring_a)
    kept_b = sums.send(kept_a[0])
    ring_a, = later_hop(2, kept_a[0], early_a, send(ring_a, ALONG), kept_a[0])
    ring_b, = later_hop(2, kept_b[0], early_b, send(ring_b, ALONG), kept_b[0])
    keep0_a, away = sums.send(ring_a)
    late_a = [send(part, WITHIN) for part in away]
    keep0_b, away = sums.send(ring_b)
    late_b = [send(part, WITHIN) for part in away]
    own_a = call_local(own_kernel, (keep0_a, late_a[4]), (None, None), [((short, breadth), I16)], "own")[0]
    beside = send(own_a, BESIDE)
    ring_a, = later_hop(3, kept_a[1], late_a, send(ring_a, ALONG), own_a)
    ring_b, = later_hop(3, kept_b[1], late_b, send(ring_b, ALONG), own_a)
    mine_a, other_a = later_hop(4, kept_a[2], late_a, send(ring_a, ALONG), own_a)
    mine_b, other_b = later_hop(4, kept_b[2], late_b, send(ring_b, ALONG), own_a)
    parts = (
        late_b[4], beside, send(mine_a, ASLANT), send(other_a, ASLANT_ACROSS), send(mine_b, ALONG), send(other_b, ACROSS),
    )
    return keep0_b, parts, mine_b


def spread(row, height):
    return jnp.concatenate([jnp.broadcast_to(row, (HEAD, row.shape[1])).astype(BF)] * (height // HEAD), axis=0)


def row_numbers(height, width):
    return lax.broadcasted_iota(jnp.int32, (height, width), 0).astype(F32).astype(BF)


GROUP = 4


def hot_kernel(places, _, col_hots, row_hots, mask):
    tile_cols = mask.shape[1] // CH
    numbers = row_numbers(GROUP * CH, GROUP * SLOTS)
    one, none = jnp.ones((), BF), jnp.zeros((), BF)
    for g in range(col_hots.shape[0]):
        part = [places[GROUP * g + n:GROUP * g + n + 1, :] for n in range(GROUP)]
        row_code = (jnp.concatenate(part, axis=1) >> 6).astype(F32)
        col_code = jnp.concatenate([(p & 63) + CH * n for n, p in enumerate(part)], axis=1).astype(F32)
        col_hots[g] = jnp.where(numbers == spread(col_code, GROUP * CH), one, none)
        row_hots[g] = jnp.where(numbers[:CH] == spread(row_code, CH), one, none)
        i, j = (GROUP * g) // tile_cols, (GROUP * g) % tile_cols
        mask[i * CH:(i + 1) * CH, j * CH:(j + GROUP) * CH] = dot_nt(row_hots[g], col_hots[g])


def pick_kernel(kept, *refs):
    parts, refs = refs[:6], refs[6:]
    momentum, places, col_hots, row_hots, mask, rows, rows_t, cols, cols_t, new_moment, payload, coef = refs
    grad = kept[...]
    for part in parts:
        grad = grad + decode(part)
    moment = 0.9 * momentum[...] + grad
    coef[...] = right_product(left_product(rows, moment), cols_t)
    tile_cols = momentum.shape[1] // CH
    for g in range(col_hots.shape[0]):
        i, j = (GROUP * g) // tile_cols, (GROUP * g) % tile_cols
        high, low = split(coef[i * CH:(i + 1) * CH, j * CH:(j + GROUP) * CH])
        chosen = dot(jnp.concatenate([high, low], axis=0), col_hots[g])
        chosen = chosen[:CH] + chosen[CH:]
        value = jnp.sum(chosen * row_hots[g].astype(F32), axis=0, keepdims=True)
        for n in range(GROUP):
            for r in range(payload.shape[0]):
                payload[r, GROUP * g + n:GROUP * g + n + 1, :] = value[:, n * SLOTS:(n + 1) * SLOTS]
    tiles = places.shape[0]
    for r in range(payload.shape[0]):
        payload[r, tiles:, :] = places[...].astype(F32)
    new_moment[...] = moment - right_product(left_product(rows_t, coef[...] * mask[...]), cols)


def decode_kernel(gathered, rows_t, cols, step_dir, total):
    reps = gathered.shape[0]
    tiles = gathered.shape[1] // 2
    tile_cols = total.shape[1] // CH
    numbers = row_numbers(CH, SLOTS)
    one, none = jnp.ones((), BF), jnp.zeros((), BF)
    parts = []
    for r in range(reps):
        high, low = split(gathered[r, :tiles, :])
        place = gathered[r, tiles:, :].astype(jnp.int32)
        parts.append([high.astype(F32), low.astype(F32), (place >> 6).astype(F32), (place & 63).astype(F32)])
    for pair in range(tiles // 2):
        blocks = []
        for t in (2 * pair, 2 * pair + 1):
            highs, lows, hots = [], [], []
            for r in range(reps):
                high, low, row_code, col_code = (spread(part[t:t + 1, :], CH) for part in parts[r])
                in_row = numbers == row_code
                highs.append(jnp.where(in_row, high, none))
                lows.append(jnp.where(in_row, low, none))
                hots.append(jnp.where(numbers == col_code, one, none))
            both = jnp.concatenate([jnp.concatenate(highs, axis=1), jnp.concatenate(lows, axis=1)], axis=0)
            out = dot_nt(both, jnp.concatenate(hots, axis=1))
            blocks.append(out[:CH] + out[CH:])
        i, j = (2 * pair) // tile_cols, (2 * pair) % tile_cols
        total[i * CH:(i + 1) * CH, j * CH:(j + 2) * CH] = jnp.concatenate(blocks, axis=1)
    decoded = right_product(left_product(rows_t, total[...]), cols)
    step_dir[...] = decoded * lax.rsqrt(decoded * decoded + 0.04)


def body(activations, out_grads, momentum, indices, counts):
    reps = lax.axis_size("rep")
    table = cosine_table(CH)
    rows = np.kron(np.eye(3), table)
    cols = np.kron(np.eye(4), table)
    rows, rows_t, cols, cols_t = (jnp.asarray(two_terms(m)) for m in (rows, rows.T, cols, cols.T))
    height, breadth = momentum.shape[1:]
    tiles = (height // CH) * (breadth // CH)
    live = lax.broadcasted_iota(jnp.int32, indices.shape[1:], 2) < counts[0]
    places = jnp.where(live, indices[0], -1).reshape(tiles, SLOTS)
    kept, parts, after = replica_sum(activations[0], out_grads[0])
    groups = tiles // GROUP
    hots = call_local(hot_kernel, (places, after), (None, ANYWHERE), [
        ((groups, GROUP * CH, GROUP * SLOTS), BF), ((groups, CH, GROUP * SLOTS), BF), ((height, breadth), F32),
    ], "hot")
    new_moment, payload = pl.pallas_call(
        pick_kernel,
        out_shape=[
            jax.ShapeDtypeStruct((height, breadth), F32),
            jax.ShapeDtypeStruct((reps, 2 * tiles, SLOTS), F32),
        ],
        scratch_shapes=[pltpu.VMEM((height, breadth), F32)],
        compiler_params=pltpu.CompilerParams(vmem_limit_bytes=32 << 20),
        name="pick",
    )(kept, *parts, momentum[0], places, *hots, rows, rows_t, cols, cols_t)
    gathered = lax.all_to_all(payload, "rep", 0, 0)
    step_dir = pl.pallas_call(
        decode_kernel,
        out_shape=jax.ShapeDtypeStruct((height, breadth), F32),
        scratch_shapes=[pltpu.VMEM((height, breadth), F32)],
        compiler_params=pltpu.CompilerParams(vmem_limit_bytes=32 << 20),
        name="decode",
    )(gathered, rows_t, cols)
    return (new_moment[None], step_dir)


def solution(mesh):
    placed = (
        P("rep", "fsdp", None),
        P("rep", "fsdp", None),
        P("rep", "fsdp", None),
        P("rep", "fsdp", None, None),
        P("rep"),
    )
    return jax.shard_map(
        body,
        mesh=mesh,
        in_specs=placed,
        out_specs=(P("rep", "fsdp", None), P("fsdp", None)),
        check_vma=False,
    )
```
